512 devices in a mesh: dp: 64 (over y, z_hi, core), tensor: 8 (over z_lo, x).
Axes of the slice: x: 4, y: 8, z: 8 (z_hi: 4, z_lo: 2; z = z_hi * 2 + z_lo), core: 2. Of those that a mesh axis runs over, the one named last changes fastest.
Arguments:
- layer_input: bfloat16 [8192, 4096], P('dp', 'tensor'), may hold values from -6 to 6
- routed_delta: bfloat16 [8192, 8, 1024], P('dp', None, 'tensor'), may hold values from -1.5 to 1.5
- shared_delta: bfloat16 [8192, 1024], P(('dp', 'tensor')), may hold values from -6 to 6
- expert_weight: bfloat16 [128, 1024, 4096], P('dp', None, 'tensor'), may hold values from -0.1875 to 0.1875
- shared_weight: bfloat16 [1024, 4096], P('dp', 'tensor'), may hold values from -0.1875 to 0.1875
- routing: int32 [8192, 8], P('dp'), may hold values from 0 to 127, all different within a row; in each aligned block of 128 rows (0 to 127, 128 to 255, ...) at most 10 rows name the same one
- slot_expert: int32 [128], replicated, may hold values from 0 to 127, each once
Outputs:
- input_gradient: bfloat16 [8192, 4096], P('dp', 'tensor')
- expert_gradient: bfloat16 [128, 1024, 4096], P('dp', None, 'tensor')
- shared_gradient: float32 [1024, 4096], P('dp', 'tensor')
The draws below stay inside these ranges and needn't reach their ends.
Inputs may be any that keep to these rules, and one draw needn't show every extreme that they name: `routing`: each row names 8 different experts; in each aligned block of 128 rows no expert is named more than 10 times, a bound that some block reaches. `slot_expert`: A permutation of the experts.
All inputs are finite; a program needn't handle non-finite values.
Results may differ from the reference program's by a relative error of at most 0.0047.
Values may be sent and summed in bfloat16 or wider, within the bound.
No kernel may reach another device: no remote copies, remote signals or barrier semaphores. Data moves between devices by JAX's collectives and lax.ppermute only.
A program may use at most 64 MiB of HBM per device.

```python
import math
import jax
import jax.numpy as jnp
import numpy as np
from jax import lax

D = 4096
H = 1024
HS = 1024
TOP = 8
TOK = 128
EXPERTS = 128
TOKENS = 8192
MOST = 10
N_DP = 64


def spiked(values, stream_key, source, target, parts, factor):
    owner, partner = [(jnp.arange(values.shape[dim]) // (values.shape[dim] // parts)).reshape([-1 if axis == dim else 1 for axis in range(values.ndim)]) for dim in (source, target)]
    chosen = jax.random.permutation(stream_key, parts)[partner]
    strong = (owner == chosen) | (owner == (partner + parts // 2) % parts)
    return jnp.where(strong, factor * values, values)


def steps_of(rng, dims, split, least, high):
    gain = 1.0
    for axis_at, parts in split:
        draws = jax.random.uniform(jax.random.fold_in(jax.random.fold_in(rng, 6), axis_at), (parts,), jnp.float32, least / len(split), high / len(split))
        gain = gain * jnp.repeat(jnp.exp(draws), dims[axis_at] // parts).reshape((-1,) + (1,) * (len(dims) - 1 - axis_at))
    return gain


def routed_block(own_key, own, number, rows, amount, top, reach, slope):
    order = jax.random.permutation(own_key, amount)
    crowded, common = load_shares(amount, rows * top, reach, slope, True), load_shares(amount, rows * top, reach, slope, False)
    places = jnp.arange(amount)

    def named(tallies, turn):
        used = int((tallies > 0).sum())
        fixed = max(1, used // 4)
        passed = fixed + (places - fixed + turn * (used - fixed)) % max(1, amount - fixed)
        return jnp.zeros((amount,), jnp.int32).at[order[jnp.where(places < fixed, places, passed)]].set(jnp.asarray(tallies, jnp.int32))

    tallies = jnp.where(number % 4 == 0, named(crowded, number // 4), named(common, number - number // 4 - 1))
    mixed = jax.random.permutation(jax.random.fold_in(own, 3), amount)
    giver, receiver = mixed[0:amount // 2 * 2:2], mixed[1:amount // 2 * 2:2]
    room = jnp.minimum(tallies[giver] - 1, reach - tallies[receiver]) // 2
    room = jnp.where((giver == order[0]) | (receiver == order[0]) | (tallies[receiver] == 0), 0, jnp.maximum(room, 0))
    passed = jax.random.randint(jax.random.fold_in(own, 4), (amount // 2,), 0, 1 << 20) % (room + 1)
    tallies = tallies.at[giver].add(-passed).at[receiver].add(passed)
    labels = jnp.searchsorted(jnp.cumsum(tallies), jnp.arange(rows * top), side="right").astype(jnp.int32)
    grid = labels.reshape(top, rows).T
    grid = grid[jax.random.permutation(jax.random.fold_in(own, 1), rows)]
    turn = jax.random.randint(jax.random.fold_in(own, 2), (rows, 1), 0, top)
    return jnp.take_along_axis(grid, (jnp.arange(top)[None, :] + turn) % top, axis=1)


def load_shares(amount, total, reach, slope, full):
    weights = [(1 << 20) // math.isqrt(standing ** slope) + 1 for standing in range(1, amount + 1)]
    largest = reach if full else min(reach, max(-(-total // amount), total * weights[0] // sum(weights)))
    least = 1 if total - largest >= amount - 1 else 0
    given, surplus = [largest] + [least] * (amount - 1), total - largest - least * (amount - 1)
    while surplus > 0:
        candidates = [i for i in range(1, amount) if given[i] < largest] or [i for i in range(1, amount) if given[i] < reach]
        mass, left = sum([weights[i] for i in candidates]), surplus
        for i in candidates:
            extra = min(reach - given[i], max(1, left * weights[i] // mass), surplus)
            given[i] = given[i] + extra
            surplus = surplus - extra
    return np.array(given)


def centred(stream_key, extent, deviation, bound, cuts=(), kind=jnp.bfloat16):
    array = jax.random.normal(stream_key, extent, jnp.float32) * deviation
    if len(cuts) > 0:
        array = steps_of(stream_key, extent, cuts, -0.22, 0.18) * array
    return jnp.clip(array, min=-bound, max=bound).astype(kind)


def heavy_noise(rng, shape, scale, reach, split, heavy, kind=jnp.bfloat16):
    drawn = scale * jax.random.normal(rng, shape, jnp.float32)
    if split:
        drawn = drawn * steps_of(rng, shape, split, -0.22, 0.18)
    return jnp.clip(spiked(drawn, jax.random.fold_in(rng, 3), *heavy), -reach, reach).astype(kind)


def setup_inputs(seed: int = 0) -> dict:
    key_of = jax.random.split(jax.random.key(seed), 8)
    layer_input = centred(key_of[0], (TOKENS, D), 1.0, 6.0, ((0, 64), (1, 8)))
    routed_delta = centred(key_of[1], (TOKENS, TOP, H), 0.25, 1.5, ((0, 64), (2, 8)))
    shared_delta = heavy_noise(key_of[2], (TOKENS, HS), 0.25, 6.0, ((0, 512),), (0, 1, 512, 6.0))
    expert_weight = centred(key_of[3], (EXPERTS, H, D), H ** -0.5, 0.1875, ((0, 64), (2, 8)))
    shared_weight = centred(key_of[4], (HS, D), HS ** -0.5, 0.1875, ((0, 64), (1, 8)))
    routing_keys = jax.random.split(jax.random.fold_in(key_of[5], 1), TOKENS // TOK)
    routing_turns = jax.random.permutation(jax.random.fold_in(key_of[5], 3), TOKENS // TOK)
    routing = jax.vmap(lambda own, number: routed_block(jax.random.fold_in(key_of[5], 2), own, number, TOK, EXPERTS, TOP, MOST, 2))(routing_keys, routing_turns).reshape((TOKENS, TOP))
    slot_expert = jax.random.permutation(key_of[6], EXPERTS).astype(jnp.int32)
    return dict(layer_input=layer_input, routed_delta=routed_delta, shared_delta=shared_delta, expert_weight=expert_weight, shared_weight=shared_weight, routing=routing, slot_expert=slot_expert)


def reference(layer_input, routed_delta, shared_delta, expert_weight, shared_weight, routing, slot_expert):
    span = N_DP * MOST
    filler = TOKENS * TOP
    flat_route = routing.reshape(-1)
    order = jnp.argsort(flat_route, stable=True).astype(jnp.int32)
    expert_ids = jnp.arange(EXPERTS, dtype=jnp.int32)
    counts = jnp.sum((flat_route[:, None] == expert_ids[None, :]).astype(jnp.int32), axis=0).astype(jnp.int32)
    starts = (jnp.cumsum(counts) - counts).astype(jnp.int32)
    order_padded = jnp.concatenate([order, jnp.full((span,), filler, jnp.int32)])
    inputs_padded = jnp.concatenate([layer_input, jnp.zeros((1, D), layer_input.dtype)], axis=0)
    deltas_padded = jnp.concatenate([routed_delta.reshape(TOKENS * TOP, H), jnp.zeros((1, H), routed_delta.dtype)], axis=0)
    lanes = jnp.arange(span, dtype=jnp.int32)

    def one_slot(total, inputs):
        expert, weight = inputs
        begin = starts[expert].astype(jnp.int32)
        picked = lax.dynamic_slice(order_padded, (begin,), (span,))
        picked = jnp.where(lanes < counts[expert], picked, filler).astype(jnp.int32)
        token_ids = (picked // TOP).astype(jnp.int32)
        rows_in = inputs_padded[token_ids]
        rows_delta = deltas_padded[picked]
        slot_gradient = jnp.dot(rows_delta.T, rows_in, preferred_element_type=jnp.float32)
        rows_out = jnp.dot(rows_delta, weight, preferred_element_type=jnp.float32).astype(jnp.bfloat16)
        rows_out = lax.optimization_barrier(rows_out).astype(jnp.float32)
        total = total.at[token_ids].add(rows_out)
        return total, slot_gradient.astype(jnp.bfloat16)

    routed, expert_gradient = lax.scan(one_slot, jnp.zeros((TOKENS + 1, D), jnp.float32), (slot_expert, expert_weight))
    shared_rows = jnp.dot(shared_delta, shared_weight, preferred_element_type=jnp.float32)
    input_gradient = (routed[:TOKENS] + shared_rows).astype(jnp.bfloat16)
    shared_gradient = jnp.dot(shared_delta.T, layer_input, preferred_element_type=jnp.float32)
    return input_gradient, expert_gradient, shared_gradient
```

```python
import functools

import jax
import jax.numpy as jnp
from jax import lax
from jax.experimental import pallas as pl
from jax.experimental.pallas import tpu as pltpu
from jax.sharding import PartitionSpec as P

MOST = 10
LANES = 128
BLOCK = 16
BF16 = jnp.bfloat16
F32 = jnp.float32
VMEM_LIMIT = 48 * 1024 * 1024


def dot(a, b, contract=((1,), (0,))):
    return lax.dot_general(a, b, (contract, ((), ())), preferred_element_type=F32)


class Plan:
    def __init__(self, slots, columns, group):
        self.slots, self.columns, self.group = slots, columns, group
        self.rows = slots * MOST
        self.padded = -(-self.rows // 8) * 8
        self.blocks = columns // LANES
        self.packed = self.blocks * self.rows
        self.slot_rows = group * MOST

    def wide_index(self, width):
        at = lax.broadcasted_iota(jnp.int32, (self.group * self.padded, width), 0)
        dest = at // self.padded
        return dest, at - dest * self.padded

    def packed_index(self, width):
        at = lax.broadcasted_iota(jnp.int32, (self.group * self.packed, width), 0)
        dest = at // self.packed
        at = at - dest * self.packed
        block = at // self.rows
        return dest, block, at - block * self.rows

    def expand(self, dest, at):
        slot = lax.broadcasted_iota(jnp.int32, dest.shape, 1)
        return one_hot(slot == jnp.where(at < self.rows, dest * self.slots + at // MOST, -1))

    def rank(self, at):
        return jnp.where(at < self.rows, at % MOST, -5).astype(F32)

    def slot_from_wide(self):
        shape = (self.slots * self.slot_rows, self.group * self.padded)
        at = lax.broadcasted_iota(jnp.int32, shape, 0)
        slot = at // self.slot_rows
        at = at - slot * self.slot_rows
        source = (at // MOST) * self.padded + slot * MOST + at % MOST
        return one_hot(lax.broadcasted_iota(jnp.int32, shape, 1) == source)

    def packed_from_slot(self):
        dest, _, at = self.packed_index(self.slots * self.slot_rows)
        source = (at // MOST) * self.slot_rows + dest * MOST + at % MOST
        return one_hot(lax.broadcasted_iota(jnp.int32, dest.shape, 1) == source)

    def block_mask(self):
        _, block, _ = self.packed_index(self.columns)
        return one_hot(lax.broadcasted_iota(jnp.int32, block.shape, 1) // LANES == block)


def one_hot(hit):
    return jnp.where(hit, 1.0, 0.0).astype(BF16)


ANYWHERE = pl.BlockSpec(memory_space=pl.ANY)
IN_VMEM = pl.BlockSpec(memory_space=pltpu.VMEM)
IN_SMEM = pl.BlockSpec(memory_space=pltpu.SMEM)


def call(kernel, outs, *args, index=(), scratch=(), after=()):
    given = len(index) + len(args)

    def run(*refs):
        kernel(*refs[:given], *refs[given + len(after) :])

    return pl.pallas_call(
        run,
        out_shape=outs,
        in_specs=[IN_SMEM] * len(index) + [IN_VMEM] * len(args) + [ANYWHERE] * len(after),
        scratch_shapes=list(scratch),
        compiler_params=pltpu.CompilerParams(vmem_limit_bytes=VMEM_LIMIT),
    )(*index, *args, *after)


def ready(values, after):
    return pl.pallas_call(
        lambda *refs: None,
        out_shape=tuple(jax.ShapeDtypeStruct(v.shape, v.dtype) for v in values),
        in_specs=[ANYWHERE] * (len(values) + len(after)),
        out_specs=tuple(ANYWHERE for _ in values),
        input_output_aliases={i: i for i in range(len(values))},
    )(*values, *after)


def select_deltas(plan, groups, top, route_ref, slot_ref, delta_ref, out_ref, place_ref):
    flat = route_ref.shape[1]
    tokens = flat // top
    hit = slot_ref[...] == route_ref[...]
    spread = one_hot(
        lax.broadcasted_iota(jnp.int32, (tokens, flat), 0) == lax.broadcasted_iota(jnp.int32, (tokens, flat), 1) // top
    )
    member = dot(one_hot(hit), spread, ((1,), (1,)))
    before = one_hot(
        lax.broadcasted_iota(jnp.int32, (tokens, tokens), 0) < lax.broadcasted_iota(jnp.int32, (tokens, tokens), 1)
    )
    ahead = dot(member.astype(BF16), before)
    place_ref[...] = jnp.where(member > 0.5, ahead, -1.0).astype(BF16)
    place_flat = jnp.where(hit, dot(ahead.astype(BF16), spread), -1.0).astype(BF16)
    slots, rows = plan.group * plan.slots, plan.group * plan.padded
    expand = plan.expand(*plan.wide_index(slots))
    rank = plan.rank(plan.wide_index(1)[1])
    for g in range(groups):
        value = dot(expand, place_flat[g * slots : (g + 1) * slots])
        out_ref[g * rows : (g + 1) * rows, :] = dot(one_hot(value == rank), delta_ref[...]).astype(BF16)


def by_block(plan, wide, block):
    total = wide[:, :LANES]
    for c in range(1, plan.blocks):
        total = jnp.where(block == c, wide[:, c * LANES : (c + 1) * LANES], total)
    return total.astype(BF16)


def widened(plan, packed, mask):
    return jnp.concatenate([packed] * plan.blocks, axis=1) * mask


def select_inputs(plan, groups, place_ref, input_ref, out_ref, chosen_ref):
    slots, rows = plan.group * plan.slots, plan.group * plan.packed
    dest, _, at = plan.packed_index(slots)
    expand = plan.expand(dest, at)
    _, block, at = plan.packed_index(LANES)
    rank = plan.rank(at)
    for g in range(groups):
        value = dot(expand, place_ref[g * slots : (g + 1) * slots, :])
        chosen = one_hot(value == rank)
        chosen_ref[g * rows : (g + 1) * rows, :] = chosen
        out_ref[g * rows : (g + 1) * rows, :] = by_block(plan, dot(chosen, input_ref[...]), block)


def place_of(index_ref, block, size):
    return pl.ds(pl.multiple_of(index_ref[block] * size, size), size)


def shared_partial(place_ref, delta_ref, input_ref, keep_ref, give_ref, sum_ref):
    sum_ref[...] = dot(delta_ref[...], input_ref[...], ((0,), (0,)))
    core = place_ref[1]
    rows = BLOCK
    for b in range(sum_ref.shape[0] // (2 * rows)):
        at = slice(b * rows, (b + 1) * rows)
        keep_ref[at, :] = sum_ref[pl.ds(pl.multiple_of((2 * b + core) * rows, rows), rows), :]
        give_ref[at, :] = sum_ref[pl.ds(pl.multiple_of((2 * b + 1 - core) * rows, rows), rows), :]


def shared_rows(place_ref, delta_ref, weight_ref, out_ref, sorted_ref):
    for k in range(weight_ref.shape[0] // BLOCK):
        z, core = (place_ref[0] - (k // 2) % 4) & 3, place_ref[1] ^ (k % 2)
        source = pl.multiple_of((k // 8 * 8 + z * 2 + core) * BLOCK, BLOCK)
        sorted_ref[k * BLOCK : (k + 1) * BLOCK, :] = weight_ref[pl.ds(source, BLOCK), :]
    out_ref[...] = dot(delta_ref[...], sorted_ref[...])


def project(plan, groups, index_ref, *refs):
    delta_refs, (weight_ref, out_ref, slot_delta_ref, value_ref, sorted_ref) = refs[:-5], refs[-5:]
    wide_rows, rows, part = plan.group * plan.padded, plan.group * plan.packed, plan.slot_rows
    for m in range(len(delta_refs)):
        for s in range(plan.slots):
            sorted_ref[s, m * LANES : (m + 1) * LANES, :] = weight_ref[s, place_of(index_ref, m, LANES), :]
    sort = plan.slot_from_wide()
    for g in range(groups):
        delta = jnp.concatenate([ref[g * wide_rows : (g + 1) * wide_rows, :] for ref in delta_refs], axis=1)
        delta = dot(sort, delta).astype(BF16)
        for s in range(plan.slots):
            slot_delta_ref[s, g * part : (g + 1) * part, :] = delta[s * part : (s + 1) * part]
    for s in range(plan.slots):
        value_ref[s] = dot(slot_delta_ref[s], sorted_ref[s]).astype(BF16)
    unsort = plan.packed_from_slot()
    block = plan.packed_index(LANES)[1]
    for g in range(groups):
        value = jnp.concatenate([value_ref[s, g * part : (g + 1) * part, :] for s in range(plan.slots)], axis=0)
        out_ref[g * rows : (g + 1) * rows, :] = by_block(plan, dot(unsort, value), block)


def weight_gradient(plan, groups, index_ref, slot_delta_ref, input_ref, out_ref, sorted_ref):
    rows, part = plan.group * plan.packed, plan.slot_rows
    unsort = plan.packed_from_slot()
    mask = plan.block_mask()
    for g in range(groups):
        wide = widened(plan, input_ref[g * rows : (g + 1) * rows, :], mask)
        wide = dot(unsort, wide, ((0,), (0,))).astype(BF16)
        for s in range(plan.slots):
            sorted_ref[s, g * part : (g + 1) * part, :] = wide[s * part : (s + 1) * part]
    for s in range(plan.slots):
        value = dot(slot_delta_ref[s], sorted_ref[s], ((0,), (0,))).astype(BF16)
        for m in range(value.shape[0] // LANES):
            out_ref[s, place_of(index_ref, m, LANES), :] = value[m * LANES : (m + 1) * LANES]


def combine(plan, groups, returned_ref, chosen_ref, shared_ref, out_ref):
    rows = plan.group * plan.packed
    mask = plan.block_mask()
    total = shared_ref[...]
    for g in range(groups):
        at = slice(g * rows, (g + 1) * rows)
        total = total + dot(chosen_ref[at, :], widened(plan, returned_ref[at, :], mask), ((0,), (0,)))
    out_ref[...] = total.astype(BF16)


def group_sum(block, groups):
    return lax.psum_scatter(block, "dp", scatter_dimension=0, axis_index_groups=groups, tiled=True)


def moved(block, axis, target):
    return lax.ppermute(block, axis, [(i, target(i)) for i in range(lax.axis_size(axis))])


def along_x(distance):
    return lambda i: (i & 4) | ((i + distance) & 3)


def along_z(distance):
    return lambda i: (i & ~6) | ((i + 2 * distance) & 6)


def other_core(i):
    return i ^ 1


def over_tensor(block):
    copies = jnp.broadcast_to(block[None], (lax.axis_size("tensor"),) + block.shape)
    return lax.all_to_all(copies, "tensor", split_axis=0, concat_axis=0, tiled=True)


def body(layer_input, routed_delta, shared_delta, expert_weight, shared_weight, routing, slot_expert):
    tokens, top = routing.shape
    slots, hidden, columns = expert_weight.shape
    shared_hidden = shared_delta.shape[1]
    dp_count = lax.axis_size("dp")
    group = 8
    groups = dp_count // group
    plan = Plan(slots, columns, group)
    wide_rows, packed_rows = dp_count * plan.padded, dp_count * plan.packed
    along_y = [[8 * y + r for y in range(dp_count // 8)] for r in range(8)]
    mine = lax.axis_index("dp")
    my_z, my_core = (mine >> 1) & 3, mine & 1
    my_place = jnp.stack([my_z, my_core])
    own = lax.axis_index("tensor")
    holders = jnp.stack([(own & 4) ^ flip | ((own + step) & 3) for step in (0, -1, 1, 2) for flip in (0, 4)])

    def exchanged(block):
        parts = block.reshape(dp_count, -1, LANES)
        return lax.all_to_all(parts, "dp", split_axis=0, concat_axis=0, tiled=True).reshape(block.shape)

    def to_right(block):
        return moved(block, "tensor", along_x(1))

    def to_left(block):
        return moved(block, "tensor", along_x(-1))

    shared_all = over_tensor(shared_delta).reshape(tokens, shared_hidden)
    send_deltas, place = call(
        functools.partial(select_deltas, plan, groups, top),
        (
            jax.ShapeDtypeStruct((wide_rows, LANES), BF16),
            jax.ShapeDtypeStruct((slot_expert.shape[0], tokens), BF16),
        ),
        routing.reshape(1, tokens * top),
        slot_expert.reshape(-1, 1),
        routed_delta.reshape(tokens * top, LANES),
    )

    send_deltas, own_weight = ready((send_deltas, shared_weight), (shared_all,))
    arrived_deltas = exchanged(send_deltas)
    send_inputs, chosen = call(
        functools.partial(select_inputs, plan, groups),
        (
            jax.ShapeDtypeStruct((packed_rows, LANES), BF16),
            jax.ShapeDtypeStruct((packed_rows, tokens), BF16),
        ),
        place,
        layer_input,
    )
    keep, give = call(
        shared_partial,
        tuple(jax.ShapeDtypeStruct((shared_hidden // 2, columns), F32) for _ in range(2)),
        shared_all,
        layer_input,
        index=(my_place,),
        scratch=[pltpu.VMEM((shared_hidden, columns), F32)],
        after=(place,),
    )
    shared_part = keep + moved(give, "dp", other_core)
    weight_part = [own_weight] + [moved(own_weight, "dp", along_z(distance)) for distance in (1, 2, 3)]
    arrived_deltas, send_inputs, *weight_part = ready(
        (arrived_deltas, send_inputs, *weight_part), (shared_part,)
    )

    partner_deltas = moved(arrived_deltas, "tensor", lambda i: i ^ 4)
    own_left, own_right = to_right(arrived_deltas), to_left(arrived_deltas)
    partner_deltas, send_inputs, own_left = ready((partner_deltas, send_inputs, own_left), (own_right,))
    arrived_inputs = exchanged(send_inputs)
    partner_left, partner_right = to_right(partner_deltas), to_left(partner_deltas)
    deltas = [
        arrived_deltas,
        partner_deltas,
        own_left,
        partner_left,
        own_right,
        partner_right,
        to_right(own_left),
        to_left(partner_right),
    ]
    shared_part = group_sum(shared_part, along_y).reshape(4, BLOCK, columns)
    weight_part = jnp.stack(weight_part)
    weight_part = jnp.stack([weight_part, moved(weight_part, "dp", other_core)], axis=1)
    outgoing, slot_deltas = call(
        functools.partial(project, plan, groups),
        (
            jax.ShapeDtypeStruct((packed_rows, LANES), BF16),
            jax.ShapeDtypeStruct((slots, dp_count * MOST, hidden), BF16),
        ),
        *deltas,
        expert_weight,
        index=(holders,),
        scratch=[
            pltpu.VMEM((slots, dp_count * MOST, columns), BF16),
            pltpu.VMEM(expert_weight.shape, BF16),
        ],
        after=(weight_part,),
    )
    (outgoing,) = ready((outgoing,), (shared_part,))

    returned = exchanged(outgoing)
    expert_gradient = call(
        functools.partial(weight_gradient, plan, groups),
        jax.ShapeDtypeStruct(expert_weight.shape, BF16),
        slot_deltas,
        arrived_inputs,
        index=(holders,),
        scratch=[pltpu.VMEM((slots, dp_count * MOST, columns), BF16)],
    )
    shared_gradient = lax.dynamic_index_in_dim(shared_part, my_z, 0, keepdims=False)
    for distance in (1, 2, 3):
        part = lax.dynamic_index_in_dim(shared_part, (my_z + distance) & 3, 0, keepdims=False)
        shared_gradient = shared_gradient + moved(part, "dp", along_z(distance))
    weight_all = lax.all_gather(
        weight_part.reshape(8 * BLOCK, columns), "dp", axis=0, axis_index_groups=along_y, tiled=True
    )
    shared_term = call(
        shared_rows,
        jax.ShapeDtypeStruct((tokens, columns), F32),
        shared_all,
        weight_all,
        index=(my_place,),
        scratch=[pltpu.VMEM((shared_hidden, columns), BF16)],
        after=(expert_gradient, shared_gradient),
    )
    input_gradient = call(
        functools.partial(combine, plan, groups),
        jax.ShapeDtypeStruct((tokens, columns), BF16),
        returned,
        chosen,
        shared_term,
    )
    return input_gradient, expert_gradient, shared_gradient


def solution(mesh):
    return jax.shard_map(
        body,
        mesh=mesh,
        in_specs=(
            P("dp", "tensor"),
            P("dp", None, "tensor"),
            P(("dp", "tensor"), None),
            P("dp", None, "tensor"),
            P("dp", "tensor"),
            P("dp", None),
            P(),
        ),
        out_specs=(P("dp", "tensor"), P("dp", None, "tensor"), P("dp", "tensor")),
        check_vma=False,
    )
```

```python
import functools

import jax
import jax.numpy as jnp
from jax import lax
from jax.experimental import pallas as pl
from jax.experimental.pallas import tpu as pltpu
from jax.sharding import PartitionSpec as P

MOST = 10
LANES = 128
BLOCK = 16
BF16 = jnp.bfloat16
F32 = jnp.float32
VMEM_LIMIT = 48 * 1024 * 1024


def dot(a, b, contract=((1,), (0,))):
    return lax.dot_general(a, b, (contract, ((), ())), preferred_element_type=F32)


class Plan:
    def __init__(self, slots, columns, group):
        self.slots, self.columns, self.group = slots, columns, group
        self.rows = slots * MOST
        self.padded = -(-self.rows // 8) * 8
        self.blocks = columns // LANES
        self.packed = self.blocks * self.rows
        self.slot_rows = group * MOST

    def wide_index(self, width):
        at = lax.broadcasted_iota(jnp.int32, (self.group * self.padded, width), 0)
        dest = at // self.padded
        return dest, at - dest * self.padded

    def packed_index(self, width):
        at = lax.broadcasted_iota(jnp.int32, (self.group * self.packed, width), 0)
        dest = at // self.packed
        at = at - dest * self.packed
        block = at // self.rows
        return dest, block, at - block * self.rows

    def expand(self, dest, at):
        slot = lax.broadcasted_iota(jnp.int32, dest.shape, 1)
        return one_hot(slot == jnp.where(at < self.rows, dest * self.slots + at // MOST, -1))

    def rank(self, at):
        return jnp.where(at < self.rows, at % MOST, -5).astype(F32)

    def slot_from_wide(self):
        shape = (self.slots * self.slot_rows, self.group * self.padded)
        at = lax.broadcasted_iota(jnp.int32, shape, 0)
        slot = at // self.slot_rows
        at = at - slot * self.slot_rows
        source = (at // MOST) * self.padded + slot * MOST + at % MOST
        return one_hot(lax.broadcasted_iota(jnp.int32, shape, 1) == source)

    def packed_from_slot(self):
        dest, _, at = self.packed_index(self.slots * self.slot_rows)
        source = (at // MOST) * self.slot_rows + dest * MOST + at % MOST
        return one_hot(lax.broadcasted_iota(jnp.int32, dest.shape, 1) == source)

    def block_mask(self):
        _, block, _ = self.packed_index(self.columns)
        return one_hot(lax.broadcasted_iota(jnp.int32, block.shape, 1) // LANES == block)


def one_hot(hit):
    return jnp.where(hit, 1.0, 0.0).astype(BF16)


ANYWHERE = pl.BlockSpec(memory_space=pl.ANY)
IN_VMEM = pl.BlockSpec(memory_space=pltpu.VMEM)
IN_SMEM = pl.BlockSpec(memory_space=pltpu.SMEM)


def call(kernel, outs, *args, index=(), scratch=(), after=(), out_specs=None):
    given = len(index) + len(args)

    def run(*refs):
        kernel(*refs[:given], *refs[given + len(after) :])

    return pl.pallas_call(
        run,
        out_shape=outs,
        in_specs=[IN_SMEM] * len(index) + [IN_VMEM] * len(args) + [ANYWHERE] * len(after),
        out_specs=jax.tree.map(lambda _: IN_VMEM, outs) if out_specs is None else out_specs,
        scratch_shapes=list(scratch),
        compiler_params=pltpu.CompilerParams(vmem_limit_bytes=VMEM_LIMIT),
    )(*index, *args, *after)


def ready(*values):
    return pl.pallas_call(
        lambda *refs: None,
        out_shape=tuple(jax.ShapeDtypeStruct(v.shape, v.dtype) for v in values),
        in_specs=[ANYWHERE] * len(values),
        out_specs=tuple(ANYWHERE for _ in values),
        input_output_aliases={i: i for i in range(len(values))},
    )(*values)


def by_block(plan, wide, block):
    total = wide[:, :LANES]
    for c in range(1, plan.blocks):
        total = jnp.where(block == c, wide[:, c * LANES : (c + 1) * LANES], total)
    return total.astype(BF16)


def widened(plan, packed, mask):
    return jnp.concatenate([packed] * plan.blocks, axis=1) * mask


def places(route_ref, slot_ref):
    top, tokens = route_ref.shape
    flat = tokens * top
    spread = lax.broadcasted_iota(jnp.int32, (tokens, flat), 0) == lax.broadcasted_iota(jnp.int32, (tokens, flat), 1) // top
    tiled = one_hot(
        lax.broadcasted_iota(jnp.int32, (top, flat), 0) == lax.broadcasted_iota(jnp.int32, (top, flat), 1) % top
    )
    routes = dot(route_ref[...].astype(F32).astype(BF16), tiled, ((0,), (0,)))
    route_row = jnp.sum(jnp.where(spread, routes, 0.0), axis=0, keepdims=True)
    spread = one_hot(spread)
    shape = (slot_ref.shape[1], slot_ref.shape[1])
    same = lax.broadcasted_iota(jnp.int32, shape, 0) == lax.broadcasted_iota(jnp.int32, shape, 1)
    slot_column = jnp.sum(jnp.where(same, slot_ref[...].astype(F32), 0.0), axis=1, keepdims=True)
    hit = slot_column == route_row
    member = dot(one_hot(hit), spread, ((1,), (1,)))
    before = one_hot(
        lax.broadcasted_iota(jnp.int32, (tokens, tokens), 0) < lax.broadcasted_iota(jnp.int32, (tokens, tokens), 1)
    )
    ahead = dot(member.astype(BF16), before)
    place = jnp.where(member > 0.5, ahead, -1.0).astype(BF16)
    place_flat = jnp.where(hit, dot(ahead.astype(BF16), spread), -1.0).astype(BF16)
    return place, place_flat


def prepare(
    plan, groups,
    route_ref, slot_ref, delta_ref, input_ref, shared_ref,
    out_ref, shared_out_ref,
):
    shared_out_ref[...] = shared_ref[...]
    place, place_flat = places(route_ref, slot_ref)
    slots, rows, dests = plan.group * plan.slots, plan.group * plan.packed, plan.group
    wide_expand = plan.expand(*plan.wide_index(slots))
    wide_rank = plan.rank(plan.wide_index(1)[1])
    dest, _, at = plan.packed_index(slots)
    packed_expand = plan.expand(dest, at)
    _, block, at = plan.packed_index(LANES)
    packed_rank = plan.rank(at)
    for g in range(groups):
        value = dot(packed_expand, place[g * slots : (g + 1) * slots])
        chosen = one_hot(value == packed_rank)
        picked = by_block(plan, dot(chosen, input_ref[...]), block)
        out_ref[g * dests : (g + 1) * dests, : plan.packed, :] = picked.reshape(dests, plan.packed, LANES)
        value = dot(wide_expand, place_flat[g * slots : (g + 1) * slots])
        picked = dot(one_hot(value == wide_rank), delta_ref[...]).astype(BF16)
        out_ref[g * dests : (g + 1) * dests, plan.packed :, :] = picked.reshape(dests, plan.padded, LANES)


def place_at(block, size):
    return pl.ds(pl.multiple_of(block * size, size), size)


def place_of(index_ref, block, size):
    return place_at(index_ref[block], size)


def shared_partial(place_ref, holder_ref, *refs):
    part_refs, (input_ref, weight_ref, all_ref, keep_ref, give_ref, weight_out_ref, sum_ref) = refs[:-7], refs[-7:]
    weight_out_ref[...] = weight_ref[...]
    for m, ref in enumerate(part_refs):
        all_ref[place_of(holder_ref, m, BLOCK), :] = ref[...]
    sum_ref[...] = dot(all_ref[...], input_ref[...], ((0,), (0,)))
    core = place_ref[1]
    for b in range(sum_ref.shape[0] // (2 * BLOCK)):
        at = slice(b * BLOCK, (b + 1) * BLOCK)
        keep_ref[at, :] = sum_ref[place_at(2 * b + core, BLOCK), :]
        give_ref[at, :] = sum_ref[place_at(2 * b + 1 - core, BLOCK), :]


def join_along_y(place_ref, part_ref, weight_ref, *refs):
    out_refs, sum_ref = refs[:-1], refs[-1]
    rows = sum_ref.shape[0]
    total = part_ref[0, :rows, :].astype(F32)
    for y in range(1, part_ref.shape[0]):
        total = total + part_ref[y, :rows, :].astype(F32)
    sum_ref[...] = total
    for y in range(part_ref.shape[0]):
        weight_ref[y * rows : (y + 1) * rows, :] = part_ref[y, rows:, :]
    for step, ref in enumerate(out_refs):
        ref[...] = sum_ref[place_at((place_ref[0] + step) & 3, BLOCK), :]


def shared_rows(plan, groups, place_ref, delta_ref, weight_ref, route_ref, slot_ref, out_ref, chosen_ref, sorted_ref):
    place = places(route_ref, slot_ref)[0]
    slots, rows = plan.group * plan.slots, plan.group * plan.packed
    dest, _, at = plan.packed_index(slots)
    expand, rank = plan.expand(dest, at), plan.rank(plan.packed_index(LANES)[2])
    for g in range(groups):
        value = dot(expand, place[g * slots : (g + 1) * slots])
        chosen_ref[g * rows : (g + 1) * rows, :] = one_hot(value == rank)
    for k in range(weight_ref.shape[0] // BLOCK):
        core, z = place_ref[1] ^ (k % 2), (place_ref[0] - (k // 2) % 4) & 3
        sorted_ref[k * BLOCK : (k + 1) * BLOCK, :] = weight_ref[place_at((core * 8 + k // 8) * 4 + z, BLOCK), :]
    out_ref[...] = dot(delta_ref[...], sorted_ref[...])


def arrange(plan, groups, arrived_ref, keep_ref, got_ref, *refs):
    weight_refs, (delta_ref, part_ref) = refs[:-2], refs[-2:]
    sort = plan.slot_from_wide()
    part = plan.slot_rows
    for g in range(groups):
        wide = arrived_ref[g * plan.group : (g + 1) * plan.group, plan.packed :, :]
        wide = dot(sort, wide.reshape(plan.group * plan.padded, LANES)).astype(BF16)
        for s in range(plan.slots):
            delta_ref[s, g * part : (g + 1) * part, :] = wide[s * part : (s + 1) * part]
    count = part_ref.shape[0]
    rows = keep_ref.shape[0] // count
    for y in range(count):
        at = slice(y * rows, (y + 1) * rows)
        part_ref[y, :rows, :] = (keep_ref[at, :] + got_ref[at, :]).astype(BF16)
        for step, ref in enumerate(weight_refs):
            part_ref[y, rows + step * BLOCK : rows + (step + 1) * BLOCK, :] = ref[...]


def project(plan, groups, index_ref, *refs):
    delta_refs, (weight_ref, out_ref, kept_at, value_ref, sorted_ref, sems) = refs[:-6], refs[-6:]
    copies = [pltpu.make_async_copy(ref, kept_at.at[m], sems.at[m]) for m, ref in enumerate(delta_refs)]
    for copy in copies:
        copy.start()
    rows, part = plan.group * plan.packed, plan.slot_rows
    for s in range(plan.slots):
        for m in range(len(delta_refs)):
            sorted_ref[s, m * LANES : (m + 1) * LANES, :] = weight_ref[s, place_of(index_ref, m, LANES), :]
        delta = jnp.concatenate([ref[s] for ref in delta_refs], axis=1)
        value_ref[s] = dot(delta, sorted_ref[s]).astype(BF16)
    unsort = plan.packed_from_slot()
    block = plan.packed_index(LANES)[1]
    for g in range(groups):
        value = jnp.concatenate([value_ref[s, g * part : (g + 1) * part, :] for s in range(plan.slots)], axis=0)
        out_ref[g * rows : (g + 1) * rows, :] = by_block(plan, dot(unsort, value), block)
    for copy in copies:
        copy.wait()


def weight_gradient(plan, groups, index_ref, delta_ref, input_ref, out_ref, sorted_ref):
    rows, part = plan.group * plan.packed, plan.slot_rows
    unsort = plan.packed_from_slot()
    mask = plan.block_mask()
    for g in range(groups):
        packed = input_ref[g * plan.group : (g + 1) * plan.group, : plan.packed, :].reshape(rows, LANES)
        wide = dot(unsort, widened(plan, packed, mask), ((0,), (0,))).astype(BF16)
        for s in range(plan.slots):
            sorted_ref[s, g * part : (g + 1) * part, :] = wide[s * part : (s + 1) * part]
    for s in range(plan.slots):
        delta = jnp.concatenate([delta_ref[m, s] for m in range(delta_ref.shape[0])], axis=1)
        value = dot(delta, sorted_ref[s], ((0,), (0,))).astype(BF16)
        for m in range(delta_ref.shape[0]):
            out_ref[s, place_of(index_ref, m, LANES), :] = value[m * LANES : (m + 1) * LANES]


def combine(plan, groups, returned_ref, chosen_ref, shared_ref, *refs):
    part_refs, (out_ref, sum_ref) = refs[:4], refs[4:]
    rows = plan.group * plan.packed
    mask = plan.block_mask()
    total = shared_ref[...]
    for g in range(groups):
        at = slice(g * rows, (g + 1) * rows)
        total = total + dot(chosen_ref[at, :], widened(plan, returned_ref[at, :], mask), ((0,), (0,)))
    out_ref[...] = total.astype(BF16)
    sum_ref[...] = part_refs[0][...] + part_refs[1][...] + part_refs[2][...] + part_refs[3][...]


def moved(block, axis, target):
    return lax.ppermute(block, axis, [(i, target(i)) for i in range(lax.axis_size(axis))])


def along_x(distance):
    return lambda i: (i & 4) | ((i + distance) & 3)


def other_z(i):
    return i ^ 4


def along_z(distance):
    return lambda i: (i & ~6) | ((i + 2 * distance) & 6)


def other_core(i):
    return i ^ 1


def to_right(block):
    return moved(block, "tensor", along_x(1))


def to_left(block):
    return moved(block, "tensor", along_x(-1))


def body(layer_input, routed_delta, shared_delta, expert_weight, shared_weight, routing, slot_expert):
    tokens, top = routing.shape
    slots, hidden, columns = expert_weight.shape
    shared_hidden = shared_delta.shape[1]
    dp_count = lax.axis_size("dp")
    group = 8
    groups = dp_count // group
    plan = Plan(slots, columns, group)
    packed_rows = dp_count * plan.packed
    mine = lax.axis_index("dp")
    my_place = jnp.stack([(mine >> 1) & 3, mine & 1])
    along_y = [[8 * y + r for y in range(dp_count // 8)] for r in range(8)]
    own = lax.axis_index("tensor")
    holders = jnp.stack([(own & 4) ^ flip | ((own + step) & 3) for step in (0, -1, 1, 2) for flip in (0, 4)])
    value_rows = pltpu.VMEM((slots, dp_count * MOST, columns), BF16)

    def exchanged(block, groups=None):
        return lax.all_to_all(block, "dp", split_axis=0, concat_axis=0, axis_index_groups=groups, tiled=True)

    sent, own_delta = call(
        functools.partial(prepare, plan, groups),
        (
            jax.ShapeDtypeStruct((dp_count, plan.packed + plan.padded, LANES), BF16),
            jax.ShapeDtypeStruct(shared_delta.shape, BF16),
        ),
        routing.T,
        slot_expert.reshape(1, -1),
        routed_delta.reshape(tokens * top, LANES),
        layer_input,
        shared_delta,
    )
    sent, other_delta = ready(sent, moved(shared_delta, "tensor", other_z))
    arrived = exchanged(sent)

    pair = (own_delta, other_delta)
    shared_all, keep, give, own_weight = call(
        shared_partial,
        (
            jax.ShapeDtypeStruct((tokens, shared_hidden), BF16),
            jax.ShapeDtypeStruct((shared_hidden // 2, columns), F32),
            jax.ShapeDtypeStruct((shared_hidden // 2, columns), F32),
            jax.ShapeDtypeStruct(shared_weight.shape, BF16),
        ),
        *pair,
        *[to_right(part) for part in pair],
        *[to_left(part) for part in pair],
        *[moved(part, "tensor", along_x(2)) for part in pair],
        layer_input,
        shared_weight,
        index=(my_place, holders),
        scratch=[pltpu.VMEM((shared_hidden, columns), F32)],
    )
    got = moved(give, "dp", other_core)
    weights = [own_weight] + [moved(own_weight, "dp", along_z(step)) for step in (1, 2, 3)]

    own_deltas, parts = call(
        functools.partial(arrange, plan, groups),
        (
            jax.ShapeDtypeStruct((slots, dp_count * MOST, LANES), BF16),
            jax.ShapeDtypeStruct((8, 8 * BLOCK, columns), BF16),
        ),
        arrived,
        keep,
        got,
        *weights,
    )
    partner_deltas = moved(own_deltas, "tensor", other_z)
    own_left, own_right = to_right(own_deltas), to_left(own_deltas)
    partner_left, partner_right = to_right(partner_deltas), to_left(partner_deltas)
    deltas = [
        own_deltas,
        partner_deltas,
        own_left,
        partner_left,
        own_right,
        partner_right,
        to_right(own_left),
        to_left(partner_right),
    ]
    parts = exchanged(parts, along_y)
    outgoing, kept_deltas = call(
        functools.partial(project, plan, groups),
        (
            jax.ShapeDtypeStruct((packed_rows, LANES), BF16),
            jax.ShapeDtypeStruct((len(deltas),) + own_deltas.shape, BF16),
        ),
        *deltas,
        expert_weight,
        index=(holders,),
        scratch=[value_rows, pltpu.VMEM(expert_weight.shape, BF16), pltpu.SemaphoreType.DMA((len(deltas),))],
        out_specs=(IN_VMEM, ANYWHERE),
    )

    returned = exchanged(outgoing.reshape(dp_count, plan.packed, LANES)).reshape(packed_rows, LANES)
    expert_gradient = call(
        functools.partial(weight_gradient, plan, groups),
        jax.ShapeDtypeStruct(expert_weight.shape, BF16),
        kept_deltas,
        arrived,
        index=(holders,),
        scratch=[value_rows],
    )
    weight_part, *shared_parts = call(
        join_along_y,
        (jax.ShapeDtypeStruct((32 * BLOCK, columns), BF16),)
        + tuple(jax.ShapeDtypeStruct((BLOCK, columns), F32) for _ in range(4)),
        parts,
        index=(my_place,),
        scratch=[pltpu.VMEM((4 * BLOCK, columns), F32)],
    )
    weight_all = jnp.concatenate([weight_part, moved(weight_part, "dp", other_core)], axis=0)
    shared_term, chosen = call(
        functools.partial(shared_rows, plan, groups),
        (jax.ShapeDtypeStruct((tokens, columns), F32), jax.ShapeDtypeStruct((packed_rows, tokens), BF16)),
        shared_all,
        weight_all,
        routing.T,
        slot_expert.reshape(1, -1),
        index=(my_place,),
        scratch=[pltpu.VMEM((shared_hidden, columns), BF16)],
        after=(expert_gradient,),
    )
    shared_parts = shared_parts[:1] + [
        moved(part, "dp", along_z(step)) for step, part in enumerate(shared_parts) if step
    ]
    input_gradient, shared_gradient = call(
        functools.partial(combine, plan, groups),
        (
            jax.ShapeDtypeStruct((tokens, columns), BF16),
            jax.ShapeDtypeStruct(shared_weight.shape, F32),
        ),
        returned,
        chosen,
        shared_term,
        *shared_parts,
    )
    return input_gradient, expert_gradient, shared_gradient


def solution(mesh):
    return jax.shard_map(
        body,
        mesh=mesh,
        in_specs=(
            P("dp", "tensor"),
            P("dp", None, "tensor"),
            P(("dp", "tensor"), None),
            P("dp", None, "tensor"),
            P("dp", "tensor"),
            P("dp", None),
            P(),
        ),
        out_specs=(P("dp", "tensor"), P("dp", None, "tensor"), P("dp", "tensor")),
        check_vma=False,
    )
```

```python
import functools

import jax
import jax.numpy as jnp
from jax import lax
from jax.experimental import pallas as pl
from jax.experimental.pallas import tpu as pltpu
from jax.sharding import PartitionSpec as P

MOST = 10
LANES = 128
BLOCK = 16
BF16 = jnp.bfloat16
F32 = jnp.float32
VMEM_LIMIT = 20 * 1024 * 1024


def dot(a, b, contract=((1,), (0,))):
    return lax.dot_general(a, b, (contract, ((), ())), preferred_element_type=F32)


class Plan:
    def __init__(self, slots, columns, group):
        self.slots, self.columns, self.group = slots, columns, group
        self.rows = slots * MOST
        self.padded = -(-self.rows // 8) * 8
        self.blocks = columns // LANES
        self.packed = self.blocks * self.rows
        self.slot_rows = group * MOST

    def wide_index(self, width):
        at = lax.broadcasted_iota(jnp.int32, (self.group * self.padded, width), 0)
        dest = at // self.padded
        return dest, at - dest * self.padded

    def packed_index(self, width):
        at = lax.broadcasted_iota(jnp.int32, (self.group * self.packed, width), 0)
        dest = at // self.packed
        at = at - dest * self.packed
        block = at // self.rows
        return dest, block, at - block * self.rows

    def expand(self, dest, at):
        slot = lax.broadcasted_iota(jnp.int32, dest.shape, 1)
        return one_hot(slot == jnp.where(at < self.rows, dest * self.slots + at // MOST, -1))

    def rank(self, at):
        return jnp.where(at < self.rows, at % MOST, -5).astype(F32)

    def slot_from_wide(self):
        shape = (self.slots * self.slot_rows, self.group * self.padded)
        at = lax.broadcasted_iota(jnp.int32, shape, 0)
        slot = at // self.slot_rows
        at = at - slot * self.slot_rows
        source = (at // MOST) * self.padded + slot * MOST + at % MOST
        return one_hot(lax.broadcasted_iota(jnp.int32, shape, 1) == source)

    def packed_from_slot(self):
        dest, _, at = self.packed_index(self.slots * self.slot_rows)
        source = (at // MOST) * self.slot_rows + dest * MOST + at % MOST
        return one_hot(lax.broadcasted_iota(jnp.int32, dest.shape, 1) == source)

    def block_mask(self):
        _, block, _ = self.packed_index(self.columns)
        return one_hot(lax.broadcasted_iota(jnp.int32, block.shape, 1) // LANES == block)


def one_hot(hit):
    return jnp.where(hit, 1.0, 0.0).astype(BF16)


ANYWHERE = pl.BlockSpec(memory_space=pl.ANY)
IN_VMEM = pl.BlockSpec(memory_space=pltpu.VMEM)
IN_SMEM = pl.BlockSpec(memory_space=pltpu.SMEM)


def call(kernel, outs, *args, index=(), scratch=(), after=(), out_specs=None):
    given = len(index) + len(args)

    def run(*refs):
        kernel(*refs[:given], *refs[given + len(after) :])

    return pl.pallas_call(
        run,
        out_shape=outs,
        in_specs=[IN_SMEM] * len(index) + [IN_VMEM] * len(args) + [ANYWHERE] * len(after),
        out_specs=jax.tree.map(lambda _: IN_VMEM, outs) if out_specs is None else out_specs,
        scratch_shapes=list(scratch),
        compiler_params=pltpu.CompilerParams(vmem_limit_bytes=VMEM_LIMIT),
    )(*index, *args, *after)


def started(pairs, semaphores):
    copies = [pltpu.make_async_copy(*pair, semaphores.at[i]) for i, pair in enumerate(pairs)]
    for copy in copies:
        copy.start()
    return copies


def ready(*values):
    return pl.pallas_call(
        lambda *refs: None,
        out_shape=tuple(jax.ShapeDtypeStruct(v.shape, v.dtype) for v in values),
        in_specs=[ANYWHERE] * len(values),
        out_specs=tuple(ANYWHERE for _ in values),
        input_output_aliases={i: i for i in range(len(values))},
    )(*values)


def by_block(plan, wide, block):
    total = wide[:, :LANES]
    for c in range(1, plan.blocks):
        total = jnp.where(block == c, wide[:, c * LANES : (c + 1) * LANES], total)
    return total.astype(BF16)


def widened(plan, packed, mask):
    return jnp.concatenate([packed] * plan.blocks, axis=1) * mask


def places(route_ref, slot_ref):
    top, tokens = route_ref.shape
    flat = tokens * top
    spread = lax.broadcasted_iota(jnp.int32, (tokens, flat), 0) == lax.broadcasted_iota(jnp.int32, (tokens, flat), 1) // top
    tiled = one_hot(
        lax.broadcasted_iota(jnp.int32, (top, flat), 0) == lax.broadcasted_iota(jnp.int32, (top, flat), 1) % top
    )
    routes = dot(route_ref[...].astype(F32).astype(BF16), tiled, ((0,), (0,)))
    route_row = jnp.sum(jnp.where(spread, routes, 0.0), axis=0, keepdims=True)
    spread = one_hot(spread)
    shape = (slot_ref.shape[1], slot_ref.shape[1])
    same = lax.broadcasted_iota(jnp.int32, shape, 0) == lax.broadcasted_iota(jnp.int32, shape, 1)
    slot_column = jnp.sum(jnp.where(same, slot_ref[...].astype(F32), 0.0), axis=1, keepdims=True)
    hit = slot_column == route_row
    member = dot(one_hot(hit), spread, ((1,), (1,)))
    before = one_hot(
        lax.broadcasted_iota(jnp.int32, (tokens, tokens), 0) < lax.broadcasted_iota(jnp.int32, (tokens, tokens), 1)
    )
    ahead = dot(member.astype(BF16), before)
    place = jnp.where(member > 0.5, ahead, -1.0).astype(BF16)
    place_flat = jnp.where(hit, dot(ahead.astype(BF16), spread), -1.0).astype(BF16)
    return place, place_flat


def prepare(
    plan, groups,
    route_ref, slot_ref, delta_ref, input_ref,
    out_ref,
):
    place, place_flat = places(route_ref, slot_ref)
    slots, rows, dests = plan.group * plan.slots, plan.group * plan.packed, plan.group
    wide_expand = plan.expand(*plan.wide_index(slots))
    wide_rank = plan.rank(plan.wide_index(1)[1])
    dest, _, at = plan.packed_index(slots)
    packed_expand = plan.expand(dest, at)
    _, block, at = plan.packed_index(LANES)
    packed_rank = plan.rank(at)
    low, odd = block < 2, block % 2 == 1
    halves = jnp.concatenate([input_ref[:, : 2 * LANES], input_ref[:, 2 * LANES :]], axis=0)
    for g in range(groups):
        hit = dot(packed_expand, place[g * slots : (g + 1) * slots]) == packed_rank
        chosen = jnp.concatenate([one_hot(hit & low), one_hot(hit & ~low)], axis=1)
        picked = dot(chosen, halves)
        picked = jnp.where(odd, picked[:, LANES:], picked[:, :LANES]).astype(BF16)
        out_ref[g * dests : (g + 1) * dests, : plan.packed, :] = picked.reshape(dests, plan.packed, LANES)
        value = dot(wide_expand, place_flat[g * slots : (g + 1) * slots])
        picked = dot(one_hot(value == wide_rank), delta_ref[...]).astype(BF16)
        out_ref[g * dests : (g + 1) * dests, plan.packed :, :] = picked.reshape(dests, plan.padded, LANES)


def place_at(block, size):
    return pl.ds(pl.multiple_of(block * size, size), size)


def place_of(index_ref, block, size):
    return place_at(index_ref[block], size)


def shared_partial(place_ref, holder_ref, *refs):
    part_refs, (input_ref, weight_ref, all_ref, keep_ref, give_ref, weight_out_ref, sum_ref) = refs[:-7], refs[-7:]
    weight_out_ref[...] = weight_ref[...]
    for m, ref in enumerate(part_refs):
        all_ref[place_of(holder_ref, m, BLOCK), :] = ref[...]
    sum_ref[...] = dot(all_ref[...], input_ref[...], ((0,), (0,)))
    core = place_ref[1]
    for b in range(sum_ref.shape[0] // (2 * BLOCK)):
        at = slice(b * BLOCK, (b + 1) * BLOCK)
        keep_ref[at, :] = sum_ref[place_at(2 * b + core, BLOCK), :]
        give_ref[at, :] = sum_ref[place_at(2 * b + 1 - core, BLOCK), :]


def join_along_y(place_ref, part_ref, weight_ref, *refs):
    out_refs, sum_ref = refs[:-1], refs[-1]
    rows = sum_ref.shape[0]
    total = part_ref[0, :rows, :].astype(F32)
    for y in range(1, part_ref.shape[0]):
        total = total + part_ref[y, :rows, :].astype(F32)
    sum_ref[...] = total
    for y in range(part_ref.shape[0]):
        weight_ref[y * rows : (y + 1) * rows, :] = part_ref[y, rows:, :]
    for step, ref in enumerate(out_refs):
        ref[...] = sum_ref[place_at((place_ref[0] + step) & 3, BLOCK), :]


def shared_rows(plan, groups, place_ref, delta_ref, weight_ref, route_ref, slot_ref, out_ref, chosen_ref, sorted_ref):
    place = places(route_ref, slot_ref)[0]
    slots, rows = plan.group * plan.slots, plan.group * plan.packed
    dest, _, at = plan.packed_index(slots)
    expand, rank = plan.expand(dest, at), plan.rank(plan.packed_index(LANES)[2])
    for g in range(groups):
        value = dot(expand, place[g * slots : (g + 1) * slots])
        chosen_ref[g * rows : (g + 1) * rows, :] = one_hot(value == rank)
    for k in range(weight_ref.shape[0] // BLOCK):
        core, z = place_ref[1] ^ (k % 2), (place_ref[0] - (k // 2) % 4) & 3
        sorted_ref[k * BLOCK : (k + 1) * BLOCK, :] = weight_ref[place_at((core * 8 + k // 8) * 4 + z, BLOCK), :]
    out_ref[...] = dot(delta_ref[...], sorted_ref[...])


def arrange(plan, groups, arrived_ref, keep_ref, got_ref, *refs):
    weight_refs, (delta_ref, part_ref) = refs[:-2], refs[-2:]
    sort = plan.slot_from_wide()
    part = plan.slot_rows
    for g in range(groups):
        wide = arrived_ref[g * plan.group : (g + 1) * plan.group, plan.packed :, :]
        wide = dot(sort, wide.reshape(plan.group * plan.padded, LANES)).astype(BF16)
        for s in range(plan.slots):
            delta_ref[s, g * part : (g + 1) * part, :] = wide[s * part : (s + 1) * part]
    count = part_ref.shape[0]
    rows = keep_ref.shape[0] // count
    for y in range(count):
        at = slice(y * rows, (y + 1) * rows)
        part_ref[y, :rows, :] = (keep_ref[at, :] + got_ref[at, :]).astype(BF16)
        for step, ref in enumerate(weight_refs):
            part_ref[y, rows + step * BLOCK : rows + (step + 1) * BLOCK, :] = ref[...]


def project_early(plan, late, index_ref, *refs):
    delta_refs, (weight_ref, out_ref, late_ref, kept_at, sorted_ref, sems) = refs[:-6], refs[-6:]
    copies = started([(ref, kept_at.at[m]) for m, ref in enumerate(delta_refs)], sems)
    count = len(delta_refs)
    for s in range(plan.slots):
        for m in range(count):
            sorted_ref[s, m * LANES : (m + 1) * LANES, :] = weight_ref[s, place_of(index_ref, m, LANES), :]
        for m in range(late):
            late_ref[s, m * LANES : (m + 1) * LANES, :] = weight_ref[s, place_of(index_ref, count + m, LANES), :]
        out_ref[s] = dot(jnp.concatenate([ref[s] for ref in delta_refs], axis=1), sorted_ref[s])
    for copy in copies:
        copy.wait()


def project(plan, groups, *refs):
    delta_refs, (weight_ref, early_ref, out_ref, kept_at, value_ref, sems) = refs[:-6], refs[-6:]
    copies = started([(ref, kept_at.at[m]) for m, ref in enumerate(delta_refs)], sems)
    rows, part = plan.group * plan.packed, plan.slot_rows
    for s in range(plan.slots):
        value = dot(jnp.concatenate([ref[s] for ref in delta_refs], axis=1), weight_ref[s])
        value_ref[s] = (early_ref[s] + value).astype(BF16)
    unsort = plan.packed_from_slot()
    block = plan.packed_index(LANES)[1]
    for g in range(groups):
        value = jnp.concatenate([value_ref[s, g * part : (g + 1) * part, :] for s in range(plan.slots)], axis=0)
        out_ref[g * rows : (g + 1) * rows, :] = by_block(plan, dot(unsort, value), block)
    for copy in copies:
        copy.wait()


def weight_gradient(plan, groups, index_ref, early_ref, late_ref, input_ref, out_ref, sorted_ref):
    rows, part = plan.group * plan.packed, plan.slot_rows
    unsort = plan.packed_from_slot()
    mask = plan.block_mask()
    for g in range(groups):
        packed = input_ref[g * plan.group : (g + 1) * plan.group, : plan.packed, :].reshape(rows, LANES)
        wide = dot(unsort, widened(plan, packed, mask), ((0,), (0,))).astype(BF16)
        for s in range(plan.slots):
            sorted_ref[s, g * part : (g + 1) * part, :] = wide[s * part : (s + 1) * part]
    for s in range(plan.slots):
        parts = [ref[m, s] for ref in (early_ref, late_ref) for m in range(ref.shape[0])]
        delta = jnp.concatenate(parts, axis=1)
        value = dot(delta, sorted_ref[s], ((0,), (0,))).astype(BF16)
        for m in range(len(parts)):
            out_ref[s, place_of(index_ref, m, LANES), :] = value[m * LANES : (m + 1) * LANES]


def combine(plan, groups, returned_ref, chosen_ref, shared_ref, *refs):
    part_refs, (out_ref, sum_ref) = refs[:4], refs[4:]
    rows = plan.group * plan.packed
    mask = plan.block_mask()
    total = shared_ref[...]
    for g in range(groups):
        at = slice(g * rows, (g + 1) * rows)
        total = total + dot(chosen_ref[at, :], widened(plan, returned_ref[at, :], mask), ((0,), (0,)))
    out_ref[...] = total.astype(BF16)
    sum_ref[...] = part_refs[0][...] + part_refs[1][...] + part_refs[2][...] + part_refs[3][...]


def moved(block, axis, target):
    return lax.ppermute(block, axis, [(i, target(i)) for i in range(lax.axis_size(axis))])


def along_x(distance):
    return lambda i: (i & 4) | ((i + distance) & 3)


def other_z(i):
    return i ^ 4


def along_z(distance):
    return lambda i: (i & ~6) | ((i + 2 * distance) & 6)


def other_core(i):
    return i ^ 1


def to_right(block):
    return moved(block, "tensor", along_x(1))


def to_left(block):
    return moved(block, "tensor", along_x(-1))


def body(layer_input, routed_delta, shared_delta, expert_weight, shared_weight, routing, slot_expert):
    tokens, top = routing.shape
    slots, hidden, columns = expert_weight.shape
    shared_hidden = shared_delta.shape[1]
    dp_count = lax.axis_size("dp")
    group = 8
    groups = dp_count // group
    plan = Plan(slots, columns, group)
    packed_rows = dp_count * plan.packed
    mine = lax.axis_index("dp")
    my_place = jnp.stack([(mine >> 1) & 3, mine & 1])
    along_y = [[8 * y + r for y in range(dp_count // 8)] for r in range(8)]
    own = lax.axis_index("tensor")
    holders = jnp.stack([(own & 4) ^ flip | ((own + step) & 3) for step in (0, -1, 1, 2) for flip in (0, 4)])
    value_rows = pltpu.VMEM((slots, dp_count * MOST, columns), BF16)

    def exchanged(block, groups=None):
        return lax.all_to_all(block, "dp", split_axis=0, concat_axis=0, axis_index_groups=groups, tiled=True)

    sent = call(
        functools.partial(prepare, plan, groups),
        jax.ShapeDtypeStruct((dp_count, plan.packed + plan.padded, LANES), BF16),
        routing.T,
        slot_expert.reshape(1, -1),
        routed_delta.reshape(tokens * top, LANES),
        layer_input,
    )
    sent, other_delta = ready(sent, moved(shared_delta, "tensor", other_z))
    arrived = exchanged(sent)

    pair = (shared_delta, other_delta)
    shared_all, keep, give, own_weight = call(
        shared_partial,
        (
            jax.ShapeDtypeStruct((tokens, shared_hidden), BF16),
            jax.ShapeDtypeStruct((shared_hidden // 2, columns), F32),
            jax.ShapeDtypeStruct((shared_hidden // 2, columns), F32),
            jax.ShapeDtypeStruct(shared_weight.shape, BF16),
        ),
        *pair,
        *[to_right(part) for part in pair],
        *[to_left(part) for part in pair],
        *[moved(part, "tensor", along_x(2)) for part in pair],
        layer_input,
        shared_weight,
        index=(my_place, holders),
        scratch=[pltpu.VMEM((shared_hidden, columns), F32)],
    )
    got = moved(give, "dp", other_core)
    weights = [own_weight] + [moved(own_weight, "dp", along_z(step)) for step in (1, 2, 3)]

    own_deltas, parts = call(
        functools.partial(arrange, plan, groups),
        (
            jax.ShapeDtypeStruct((slots, dp_count * MOST, LANES), BF16),
            jax.ShapeDtypeStruct((8, 8 * BLOCK, columns), BF16),
        ),
        arrived,
        keep,
        got,
        *weights,
    )
    partner_deltas = moved(own_deltas, "tensor", other_z)
    own_left, own_right = to_right(own_deltas), to_left(own_deltas)
    partner_left, partner_right = to_right(partner_deltas), to_left(partner_deltas)
    deltas = [
        own_deltas,
        partner_deltas,
        own_left,
        partner_left,
        own_right,
        partner_right,
        to_right(own_left),
        to_left(partner_right),
    ]
    parts = exchanged(parts, along_y)
    early, late = deltas[:6], deltas[6:]
    early_rows, late_weight, kept_early = call(
        functools.partial(project_early, plan, len(late)),
        (
            jax.ShapeDtypeStruct((slots, dp_count * MOST, columns), F32),
            jax.ShapeDtypeStruct((slots, len(late) * LANES, columns), BF16),
            jax.ShapeDtypeStruct((len(early),) + own_deltas.shape, BF16),
        ),
        *early,
        expert_weight,
        index=(holders,),
        scratch=[
            pltpu.VMEM((slots, len(early) * LANES, columns), BF16),
            pltpu.SemaphoreType.DMA((len(early),)),
        ],
        out_specs=(IN_VMEM, IN_VMEM, ANYWHERE),
    )
    outgoing, kept_late = call(
        functools.partial(project, plan, groups),
        (
            jax.ShapeDtypeStruct((packed_rows, LANES), BF16),
            jax.ShapeDtypeStruct((len(late),) + own_deltas.shape, BF16),
        ),
        *late,
        late_weight,
        early_rows,
        scratch=[value_rows, pltpu.SemaphoreType.DMA((len(late),))],
        out_specs=(IN_VMEM, ANYWHERE),
    )

    returned = exchanged(outgoing.reshape(dp_count, plan.packed, LANES)).reshape(packed_rows, LANES)
    expert_gradient = call(
        functools.partial(weight_gradient, plan, groups),
        jax.ShapeDtypeStruct(expert_weight.shape, BF16),
        kept_early,
        kept_late,
        arrived,
        index=(holders,),
        scratch=[value_rows],
    )
    weight_part, *shared_parts = call(
        join_along_y,
        (jax.ShapeDtypeStruct((32 * BLOCK, columns), BF16),)
        + tuple(jax.ShapeDtypeStruct((BLOCK, columns), F32) for _ in range(4)),
        parts,
        index=(my_place,),
        scratch=[pltpu.VMEM((4 * BLOCK, columns), F32)],
    )
    weight_all = jnp.concatenate([weight_part, moved(weight_part, "dp", other_core)], axis=0)
    shared_term, chosen = call(
        functools.partial(shared_rows, plan, groups),
        (jax.ShapeDtypeStruct((tokens, columns), F32), jax.ShapeDtypeStruct((packed_rows, tokens), BF16)),
        shared_all,
        weight_all,
        routing.T,
        slot_expert.reshape(1, -1),
        index=(my_place,),
        scratch=[pltpu.VMEM((shared_hidden, columns), BF16)],
        after=(expert_gradient,),
    )
    shared_parts = shared_parts[:1] + [
        moved(part, "dp", along_z(step)) for step, part in enumerate(shared_parts) if step
    ]
    input_gradient, shared_gradient = call(
        functools.partial(combine, plan, groups),
        (
            jax.ShapeDtypeStruct((tokens, columns), BF16),
            jax.ShapeDtypeStruct(shared_weight.shape, F32),
        ),
        returned,
        chosen,
        shared_term,
        *shared_parts,
    )
    return input_gradient, expert_gradient, shared_gradient


def solution(mesh):
    return jax.shard_map(
        body,
        mesh=mesh,
        in_specs=(
            P("dp", "tensor"),
            P("dp", None, "tensor"),
            P(("dp", "tensor"), None),
            P("dp", None, "tensor"),
            P("dp", "tensor"),
            P("dp", None),
            P(),
        ),
        out_specs=(P("dp", "tensor"), P("dp", None, "tensor"), P("dp", "tensor")),
        check_vma=False,
    )
```

```python
import functools

import jax
import jax.numpy as jnp
from jax import lax
from jax.experimental import pallas as pl
from jax.experimental.pallas import tpu as pltpu
from jax.sharding import PartitionSpec as P

MOST = 10
LANES = 128
BLOCK = 16
BF16 = jnp.bfloat16
F32 = jnp.float32
VMEM_LIMIT = 20 * 1024 * 1024


def dot(a, b, contract=((1,), (0,))):
    return lax.dot_general(a, b, (contract, ((), ())), preferred_element_type=F32)


class Plan:
    def __init__(self, slots, columns, group):
        self.slots, self.columns, self.group = slots, columns, group
        self.rows = slots * MOST
        self.padded = -(-self.rows // 8) * 8
        self.blocks = columns // LANES
        self.packed = self.blocks * self.rows
        self.slot_rows = group * MOST

    def wide_index(self, width):
        at = lax.broadcasted_iota(jnp.int32, (self.group * self.padded, width), 0)
        dest = at // self.padded
        return dest, at - dest * self.padded

    def packed_index(self, width):
        at = lax.broadcasted_iota(jnp.int32, (self.group * self.packed, width), 0)
        dest = at // self.packed
        at = at - dest * self.packed
        block = at // self.rows
        return dest, block, at - block * self.rows

    def expand(self, dest, at):
        slot = lax.broadcasted_iota(jnp.int32, dest.shape, 1)
        return one_hot(slot == jnp.where(at < self.rows, dest * self.slots + at // MOST, -1))

    def rank(self, at):
        return jnp.where(at < self.rows, at % MOST, -5).astype(F32)

    def slot_from_wide(self):
        shape = (self.slots * self.slot_rows, self.group * self.padded)
        at = lax.broadcasted_iota(jnp.int32, shape, 0)
        slot = at // self.slot_rows
        at = at - slot * self.slot_rows
        source = (at // MOST) * self.padded + slot * MOST + at % MOST
        return one_hot(lax.broadcasted_iota(jnp.int32, shape, 1) == source)

    def packed_from_slot(self):
        dest, _, at = self.packed_index(self.slots * self.slot_rows)
        source = (at // MOST) * self.slot_rows + dest * MOST + at % MOST
        return one_hot(lax.broadcasted_iota(jnp.int32, dest.shape, 1) == source)

    def block_mask(self):
        _, block, _ = self.packed_index(self.columns)
        return one_hot(lax.broadcasted_iota(jnp.int32, block.shape, 1) // LANES == block)


def one_hot(hit):
    return jnp.where(hit, 1.0, 0.0).astype(BF16)


ANYWHERE = pl.BlockSpec(memory_space=pl.ANY)
IN_VMEM = pl.BlockSpec(memory_space=pltpu.VMEM)
IN_SMEM = pl.BlockSpec(memory_space=pltpu.SMEM)


def call(kernel, outs, *args, index=(), scratch=(), after=(), out_specs=None):
    given = len(index) + len(args)

    def run(*refs):
        kernel(*refs[:given], *refs[given + len(after) :])

    return pl.pallas_call(
        run,
        out_shape=outs,
        in_specs=[IN_SMEM] * len(index) + [IN_VMEM] * len(args) + [ANYWHERE] * len(after),
        out_specs=jax.tree.map(lambda _: IN_VMEM, outs) if out_specs is None else out_specs,
        scratch_shapes=list(scratch),
        compiler_params=pltpu.CompilerParams(vmem_limit_bytes=VMEM_LIMIT),
    )(*index, *args, *after)


def started(pairs, semaphores):
    copies = [pltpu.make_async_copy(*pair, semaphores.at[i]) for i, pair in enumerate(pairs)]
    for copy in copies:
        copy.start()
    return copies


def ready(*values):
    return pl.pallas_call(
        lambda *refs: None,
        out_shape=tuple(jax.ShapeDtypeStruct(v.shape, v.dtype) for v in values),
        in_specs=[ANYWHERE] * len(values),
        out_specs=tuple(ANYWHERE for _ in values),
        input_output_aliases={i: i for i in range(len(values))},
    )(*values)


def by_block(plan, wide, block):
    total = wide[:, :LANES]
    for c in range(1, plan.blocks):
        total = jnp.where(block == c, wide[:, c * LANES : (c + 1) * LANES], total)
    return total.astype(BF16)


def widened(plan, packed, mask):
    return jnp.concatenate([packed] * plan.blocks, axis=1) * mask


def places(route_ref, slot_ref):
    top, tokens = route_ref.shape
    flat = tokens * top
    spread = lax.broadcasted_iota(jnp.int32, (tokens, flat), 0) == lax.broadcasted_iota(jnp.int32, (tokens, flat), 1) // top
    tiled = one_hot(
        lax.broadcasted_iota(jnp.int32, (top, flat), 0) == lax.broadcasted_iota(jnp.int32, (top, flat), 1) % top
    )
    routes = dot(route_ref[...].astype(F32).astype(BF16), tiled, ((0,), (0,)))
    route_row = jnp.sum(jnp.where(spread, routes, 0.0), axis=0, keepdims=True)
    spread = one_hot(spread)
    shape = (slot_ref.shape[1], slot_ref.shape[1])
    same = lax.broadcasted_iota(jnp.int32, shape, 0) == lax.broadcasted_iota(jnp.int32, shape, 1)
    slot_column = jnp.sum(jnp.where(same, slot_ref[...].astype(F32), 0.0), axis=1, keepdims=True)
    hit = slot_column == route_row
    member = dot(one_hot(hit), spread, ((1,), (1,)))
    before = one_hot(
        lax.broadcasted_iota(jnp.int32, (tokens, tokens), 0) < lax.broadcasted_iota(jnp.int32, (tokens, tokens), 1)
    )
    ahead = dot(member.astype(BF16), before)
    place = jnp.where(member > 0.5, ahead, -1.0).astype(BF16)
    place_flat = jnp.where(hit, dot(ahead.astype(BF16), spread), -1.0).astype(BF16)
    return place, place_flat


def prepare(
    plan, groups,
    route_ref, slot_ref, delta_ref, input_ref,
    out_ref,
):
    place, place_flat = places(route_ref, slot_ref)
    slots, rows, dests = plan.group * plan.slots, plan.group * plan.packed, plan.group
    wide_expand = plan.expand(*plan.wide_index(slots))
    wide_rank = plan.rank(plan.wide_index(1)[1])
    dest, _, at = plan.packed_index(slots)
    packed_expand = plan.expand(dest, at)
    _, block, at = plan.packed_index(LANES)
    packed_rank = plan.rank(at)
    low, odd = block < 2, block % 2 == 1
    halves = jnp.concatenate([input_ref[:, : 2 * LANES], input_ref[:, 2 * LANES :]], axis=0)
    for g in range(groups):
        hit = dot(packed_expand, place[g * slots : (g + 1) * slots]) == packed_rank
        chosen = jnp.concatenate([one_hot(hit & low), one_hot(hit & ~low)], axis=1)
        picked = dot(chosen, halves)
        picked = jnp.where(odd, picked[:, LANES:], picked[:, :LANES]).astype(BF16)
        out_ref[g * dests : (g + 1) * dests, : plan.packed, :] = picked.reshape(dests, plan.packed, LANES)
        value = dot(wide_expand, place_flat[g * slots : (g + 1) * slots])
        picked = dot(one_hot(value == wide_rank), delta_ref[...]).astype(BF16)
        out_ref[g * dests : (g + 1) * dests, plan.packed :, :] = picked.reshape(dests, plan.padded, LANES)


def place_at(block, size):
    return pl.ds(pl.multiple_of(block * size, size), size)


def place_of(index_ref, block, size):
    return place_at(index_ref[block], size)


def shared_partial(place_ref, holder_ref, *refs):
    part_refs, (input_ref, weight_ref, all_ref, keep_ref, give_ref, weight_out_ref, sum_ref) = refs[:-7], refs[-7:]
    weight_out_ref[...] = weight_ref[...]
    for m, ref in enumerate(part_refs):
        all_ref[place_of(holder_ref, m, BLOCK), :] = ref[...]
    sum_ref[...] = dot(all_ref[...], input_ref[...], ((0,), (0,)))
    core = place_ref[1]
    for b in range(sum_ref.shape[0] // (2 * BLOCK)):
        at = slice(b * BLOCK, (b + 1) * BLOCK)
        keep_ref[at, :] = sum_ref[place_at(2 * b + core, BLOCK), :]
        give_ref[at, :] = sum_ref[place_at(2 * b + 1 - core, BLOCK), :]


def join_along_y(place_ref, part_ref, weight_ref, *refs):
    out_refs, sum_ref = refs[:-1], refs[-1]
    rows = sum_ref.shape[0]
    total = part_ref[0, :rows, :].astype(F32)
    for y in range(1, part_ref.shape[0]):
        total = total + part_ref[y, :rows, :].astype(F32)
    sum_ref[...] = total
    for y in range(part_ref.shape[0]):
        weight_ref[y * rows : (y + 1) * rows, :] = part_ref[y, rows:, :]
    for step, ref in enumerate(out_refs):
        ref[...] = sum_ref[place_at((place_ref[0] + step) & 3, BLOCK), :]


def shared_rows(plan, groups, place_ref, delta_ref, weight_ref, route_ref, slot_ref, out_ref, chosen_ref, sorted_ref):
    place = places(route_ref, slot_ref)[0]
    slots, rows = plan.group * plan.slots, plan.group * plan.packed
    dest, _, at = plan.packed_index(slots)
    expand, rank = plan.expand(dest, at), plan.rank(plan.packed_index(LANES)[2])
    for g in range(groups):
        value = dot(expand, place[g * slots : (g + 1) * slots])
        chosen_ref[g * rows : (g + 1) * rows, :] = one_hot(value == rank)
    for k in range(weight_ref.shape[0] // BLOCK):
        core, z = place_ref[1] ^ (k % 2), (place_ref[0] - (k // 2) % 4) & 3
        sorted_ref[k * BLOCK : (k + 1) * BLOCK, :] = weight_ref[place_at((core * 8 + k // 8) * 4 + z, BLOCK), :]
    out_ref[...] = dot(delta_ref[...], sorted_ref[...])


def arrange(plan, groups, arrived_ref, shared_ref, *refs):
    weight_refs, (delta_ref, part_ref) = refs[:-2], refs[-2:]
    sort = plan.slot_from_wide()
    part = plan.slot_rows
    for g in range(groups):
        wide = arrived_ref[g * plan.group : (g + 1) * plan.group, plan.packed :, :]
        wide = dot(sort, wide.reshape(plan.group * plan.padded, LANES)).astype(BF16)
        for s in range(plan.slots):
            delta_ref[s, g * part : (g + 1) * part, :] = wide[s * part : (s + 1) * part]
    count = part_ref.shape[0]
    rows = shared_ref.shape[0] // count
    for y in range(count):
        at = slice(y * rows, (y + 1) * rows)
        part_ref[y, :rows, :] = shared_ref[at, :]
        for step, ref in enumerate(weight_refs):
            part_ref[y, rows + step * BLOCK : rows + (step + 1) * BLOCK, :] = ref[...]


def project_early(plan, late, index_ref, *refs):
    delta_refs, (weight_ref, out_ref, late_ref, kept_at, sorted_ref, sems) = refs[:-6], refs[-6:]
    copies = started([(ref, kept_at.at[m]) for m, ref in enumerate(delta_refs)], sems)
    count = len(delta_refs)
    for s in range(plan.slots):
        for m in range(count):
            sorted_ref[s, m * LANES : (m + 1) * LANES, :] = weight_ref[s, place_of(index_ref, m, LANES), :]
        for m in range(late):
            late_ref[s, m * LANES : (m + 1) * LANES, :] = weight_ref[s, place_of(index_ref, count + m, LANES), :]
        out_ref[s] = dot(jnp.concatenate([ref[s] for ref in delta_refs], axis=1), sorted_ref[s])
    for copy in copies:
        copy.wait()


def project(plan, groups, *refs):
    delta_refs, (weight_ref, early_ref, out_ref, kept_at, value_ref, sems) = refs[:-6], refs[-6:]
    copies = started([(ref, kept_at.at[m]) for m, ref in enumerate(delta_refs)], sems)
    rows, part = plan.group * plan.packed, plan.slot_rows
    for s in range(plan.slots):
        value = dot(jnp.concatenate([ref[s] for ref in delta_refs], axis=1), weight_ref[s])
        value_ref[s] = (early_ref[s] + value).astype(BF16)
    unsort = plan.packed_from_slot()
    block = plan.packed_index(LANES)[1]
    for g in range(groups):
        value = jnp.concatenate([value_ref[s, g * part : (g + 1) * part, :] for s in range(plan.slots)], axis=0)
        out_ref[g * rows : (g + 1) * rows, :] = by_block(plan, dot(unsort, value), block)
    for copy in copies:
        copy.wait()


def weight_gradient(plan, groups, index_ref, early_ref, late_ref, input_ref, out_ref, sorted_ref):
    rows, part = plan.group * plan.packed, plan.slot_rows
    unsort = plan.packed_from_slot()
    mask = plan.block_mask()
    for g in range(groups):
        packed = input_ref[g * plan.group : (g + 1) * plan.group, : plan.packed, :].reshape(rows, LANES)
        wide = dot(unsort, widened(plan, packed, mask), ((0,), (0,))).astype(BF16)
        for s in range(plan.slots):
            sorted_ref[s, g * part : (g + 1) * part, :] = wide[s * part : (s + 1) * part]
    for s in range(plan.slots):
        parts = [ref[m, s] for ref in (early_ref, late_ref) for m in range(ref.shape[0])]
        delta = jnp.concatenate(parts, axis=1)
        value = dot(delta, sorted_ref[s], ((0,), (0,))).astype(BF16)
        for m in range(len(parts)):
            out_ref[s, place_of(index_ref, m, LANES), :] = value[m * LANES : (m + 1) * LANES]


def combine(plan, groups, returned_ref, chosen_ref, shared_ref, *refs):
    part_refs, (out_ref, sum_ref) = refs[:4], refs[4:]
    rows = plan.group * plan.packed
    mask = plan.block_mask()
    total = shared_ref[...]
    for g in range(groups):
        at = slice(g * rows, (g + 1) * rows)
        total = total + dot(chosen_ref[at, :], widened(plan, returned_ref[at, :], mask), ((0,), (0,)))
    out_ref[...] = total.astype(BF16)
    sum_ref[...] = part_refs[0][...] + part_refs[1][...] + part_refs[2][...] + part_refs[3][...]


def moved(block, axis, target):
    return lax.ppermute(block, axis, [(i, target(i)) for i in range(lax.axis_size(axis))])


def along_x(distance):
    return lambda i: (i & 4) | ((i + distance) & 3)


def other_z(i):
    return i ^ 4


def along_z(distance):
    return lambda i: (i & ~6) | ((i + 2 * distance) & 6)


def other_core(i):
    return i ^ 1


def to_right(block):
    return moved(block, "tensor", along_x(1))


def to_left(block):
    return moved(block, "tensor", along_x(-1))


def body(layer_input, routed_delta, shared_delta, expert_weight, shared_weight, routing, slot_expert):
    tokens, top = routing.shape
    slots, hidden, columns = expert_weight.shape
    shared_hidden = shared_delta.shape[1]
    dp_count = lax.axis_size("dp")
    group = 8
    groups = dp_count // group
    plan = Plan(slots, columns, group)
    packed_rows = dp_count * plan.packed
    mine = lax.axis_index("dp")
    my_place = jnp.stack([(mine >> 1) & 3, mine & 1])
    along_y = [[8 * y + r for y in range(dp_count // 8)] for r in range(8)]
    own = lax.axis_index("tensor")
    holders = jnp.stack([(own & 4) ^ flip | ((own + step) & 3) for step in (0, -1, 1, 2) for flip in (0, 4)])
    value_rows = pltpu.VMEM((slots, dp_count * MOST, columns), BF16)

    def exchanged(block, groups=None):
        return lax.all_to_all(block, "dp", split_axis=0, concat_axis=0, axis_index_groups=groups, tiled=True)

    sent = call(
        functools.partial(prepare, plan, groups),
        jax.ShapeDtypeStruct((dp_count, plan.packed + plan.padded, LANES), BF16),
        routing.T,
        slot_expert.reshape(1, -1),
        routed_delta.reshape(tokens * top, LANES),
        layer_input,
    )
    sent, other_delta = ready(sent, moved(shared_delta, "tensor", other_z))
    arrived = exchanged(sent)

    pair = (shared_delta, other_delta)
    shared_all, keep, give, own_weight = call(
        shared_partial,
        (
            jax.ShapeDtypeStruct((tokens, shared_hidden), BF16),
            jax.ShapeDtypeStruct((shared_hidden // 2, columns), F32),
            jax.ShapeDtypeStruct((shared_hidden // 2, columns), F32),
            jax.ShapeDtypeStruct(shared_weight.shape, BF16),
        ),
        *pair,
        *[to_right(part) for part in pair],
        *[to_left(part) for part in pair],
        *[moved(part, "tensor", along_x(2)) for part in pair],
        layer_input,
        shared_weight,
        index=(my_place, holders),
        scratch=[pltpu.VMEM((shared_hidden, columns), F32)],
    )
    shared_part = (keep + moved(give, "dp", other_core)).astype(BF16)
    weights = [own_weight] + [moved(own_weight, "dp", along_z(step)) for step in (1, 2, 3)]

    own_deltas, parts = call(
        functools.partial(arrange, plan, groups),
        (
            jax.ShapeDtypeStruct((slots, dp_count * MOST, LANES), BF16),
            jax.ShapeDtypeStruct((8, 8 * BLOCK, columns), BF16),
        ),
        arrived,
        shared_part,
        *weights,
    )
    partner_deltas = moved(own_deltas, "tensor", other_z)
    own_left, own_right = to_right(own_deltas), to_left(own_deltas)
    partner_left, partner_right = to_right(partner_deltas), to_left(partner_deltas)
    deltas = [
        own_deltas,
        partner_deltas,
        own_left,
        partner_left,
        own_right,
        partner_right,
        to_right(own_left),
        to_left(partner_right),
    ]
    parts = exchanged(parts, along_y)
    early, late = deltas[:6], deltas[6:]
    early_rows, late_weight, kept_early = call(
        functools.partial(project_early, plan, len(late)),
        (
            jax.ShapeDtypeStruct((slots, dp_count * MOST, columns), F32),
            jax.ShapeDtypeStruct((slots, len(late) * LANES, columns), BF16),
            jax.ShapeDtypeStruct((len(early),) + own_deltas.shape, BF16),
        ),
        *early,
        expert_weight,
        index=(holders,),
        scratch=[
            pltpu.VMEM((slots, len(early) * LANES, columns), BF16),
            pltpu.SemaphoreType.DMA((len(early),)),
        ],
        out_specs=(IN_VMEM, IN_VMEM, ANYWHERE),
    )
    outgoing, kept_late = call(
        functools.partial(project, plan, groups),
        (
            jax.ShapeDtypeStruct((packed_rows, LANES), BF16),
            jax.ShapeDtypeStruct((len(late),) + own_deltas.shape, BF16),
        ),
        *late,
        late_weight,
        early_rows,
        scratch=[value_rows, pltpu.SemaphoreType.DMA((len(late),))],
        out_specs=(IN_VMEM, ANYWHERE),
    )

    returned = exchanged(outgoing.reshape(dp_count, plan.packed, LANES)).reshape(packed_rows, LANES)
    expert_gradient = call(
        functools.partial(weight_gradient, plan, groups),
        jax.ShapeDtypeStruct(expert_weight.shape, BF16),
        kept_early,
        kept_late,
        arrived,
        index=(holders,),
        scratch=[value_rows],
    )
    weight_part, *shared_parts = call(
        join_along_y,
        (jax.ShapeDtypeStruct((32 * BLOCK, columns), BF16),)
        + tuple(jax.ShapeDtypeStruct((BLOCK, columns), F32) for _ in range(4)),
        parts,
        index=(my_place,),
        scratch=[pltpu.VMEM((4 * BLOCK, columns), F32)],
    )
    weight_all = jnp.concatenate([weight_part, moved(weight_part, "dp", other_core)], axis=0)
    shared_term, chosen = call(
        functools.partial(shared_rows, plan, groups),
        (jax.ShapeDtypeStruct((tokens, columns), F32), jax.ShapeDtypeStruct((packed_rows, tokens), BF16)),
        shared_all,
        weight_all,
        routing.T,
        slot_expert.reshape(1, -1),
        index=(my_place,),
        scratch=[pltpu.VMEM((shared_hidden, columns), BF16)],
        after=(expert_gradient,),
    )
    shared_parts = shared_parts[:1] + [
        moved(part, "dp", along_z(step)) for step, part in enumerate(shared_parts) if step
    ]
    input_gradient, shared_gradient = call(
        functools.partial(combine, plan, groups),
        (
            jax.ShapeDtypeStruct((tokens, columns), BF16),
            jax.ShapeDtypeStruct(shared_weight.shape, F32),
        ),
        returned,
        chosen,
        shared_term,
        *shared_parts,
    )
    return input_gradient, expert_gradient, shared_gradient


def solution(mesh):
    return jax.shard_map(
        body,
        mesh=mesh,
        in_specs=(
            P("dp", "tensor"),
            P("dp", None, "tensor"),
            P(("dp", "tensor"), None),
            P("dp", None, "tensor"),
            P("dp", "tensor"),
            P("dp", None),
            P(),
        ),
        out_specs=(P("dp", "tensor"), P("dp", None, "tensor"), P("dp", "tensor")),
        check_vma=False,
    )
```

```python
import functools

import jax
import jax.numpy as jnp
from jax import lax
from jax.experimental import pallas as pl
from jax.experimental.pallas import tpu as pltpu
from jax.sharding import PartitionSpec as P

MOST = 10
LANES = 128
BLOCK = 16
BF16 = jnp.bfloat16
F32 = jnp.float32
VMEM_LIMIT = 20 * 1024 * 1024


def dot(a, b, contract=((1,), (0,))):
    return lax.dot_general(a, b, (contract, ((), ())), preferred_element_type=F32)


class Plan:
    def __init__(self, slots, columns, group):
        self.slots, self.columns, self.group = slots, columns, group
        self.rows = slots * MOST
        self.padded = -(-self.rows // 8) * 8
        self.blocks = columns // LANES
        self.packed = self.blocks * self.rows
        self.slot_rows = group * MOST

    def wide_index(self, width):
        at = lax.broadcasted_iota(jnp.int32, (self.group * self.padded, width), 0)
        dest = at // self.padded
        return dest, at - dest * self.padded

    def packed_index(self, width):
        at = lax.broadcasted_iota(jnp.int32, (self.group * self.packed, width), 0)
        dest = at // self.packed
        at = at - dest * self.packed
        block = at // self.rows
        return dest, block, at - block * self.rows

    def expand(self, dest, at):
        slot = lax.broadcasted_iota(jnp.int32, dest.shape, 1)
        return one_hot(slot == jnp.where(at < self.rows, dest * self.slots + at // MOST, -1))

    def rank(self, at):
        return jnp.where(at < self.rows, at % MOST, -5).astype(F32)

    def slot_from_wide(self):
        shape = (self.slots * self.slot_rows, self.group * self.padded)
        at = lax.broadcasted_iota(jnp.int32, shape, 0)
        slot = at // self.slot_rows
        at = at - slot * self.slot_rows
        source = (at // MOST) * self.padded + slot * MOST + at % MOST
        return one_hot(lax.broadcasted_iota(jnp.int32, shape, 1) == source)

    def packed_from_slot(self):
        dest, _, at = self.packed_index(self.slots * self.slot_rows)
        source = (at // MOST) * self.slot_rows + dest * MOST + at % MOST
        return one_hot(lax.broadcasted_iota(jnp.int32, dest.shape, 1) == source)

    def block_mask(self):
        _, block, _ = self.packed_index(self.columns)
        return one_hot(lax.broadcasted_iota(jnp.int32, block.shape, 1) // LANES == block)


def one_hot(hit):
    return jnp.where(hit, 1.0, 0.0).astype(BF16)


ANYWHERE = pl.BlockSpec(memory_space=pl.ANY)
IN_VMEM = pl.BlockSpec(memory_space=pltpu.VMEM)
IN_SMEM = pl.BlockSpec(memory_space=pltpu.SMEM)


def call(kernel, outs, *args, index=(), scratch=(), after=(), out_specs=None):
    given = len(index) + len(args)

    def run(*refs):
        kernel(*refs[:given], *refs[given + len(after) :])

    return pl.pallas_call(
        run,
        out_shape=outs,
        in_specs=[IN_SMEM] * len(index) + [IN_VMEM] * len(args) + [ANYWHERE] * len(after),
        out_specs=jax.tree.map(lambda _: IN_VMEM, outs) if out_specs is None else out_specs,
        scratch_shapes=list(scratch),
        compiler_params=pltpu.CompilerParams(vmem_limit_bytes=VMEM_LIMIT),
    )(*index, *args, *after)


def started(pairs, semaphores):
    copies = [pltpu.make_async_copy(*pair, semaphores.at[i]) for i, pair in enumerate(pairs)]
    for copy in copies:
        copy.start()
    return copies


def ready(*values):
    return pl.pallas_call(
        lambda *refs: None,
        out_shape=tuple(jax.ShapeDtypeStruct(v.shape, v.dtype) for v in values),
        in_specs=[ANYWHERE] * len(values),
        out_specs=tuple(ANYWHERE for _ in values),
        input_output_aliases={i: i for i in range(len(values))},
    )(*values)


def by_block(plan, wide, block):
    total = wide[:, :LANES]
    for c in range(1, plan.blocks):
        total = jnp.where(block == c, wide[:, c * LANES : (c + 1) * LANES], total)
    return total.astype(BF16)


def widened(plan, packed, mask):
    return jnp.concatenate([packed] * plan.blocks, axis=1) * mask


def places(route_ref, slot_ref):
    top, tokens = route_ref.shape
    flat = tokens * top
    spread = lax.broadcasted_iota(jnp.int32, (tokens, flat), 0) == lax.broadcasted_iota(jnp.int32, (tokens, flat), 1) // top
    tiled = one_hot(
        lax.broadcasted_iota(jnp.int32, (top, flat), 0) == lax.broadcasted_iota(jnp.int32, (top, flat), 1) % top
    )
    routes = dot(route_ref[...].astype(F32).astype(BF16), tiled, ((0,), (0,)))
    route_row = jnp.sum(jnp.where(spread, routes, 0.0), axis=0, keepdims=True)
    spread = one_hot(spread)
    shape = (slot_ref.shape[1], slot_ref.shape[1])
    same = lax.broadcasted_iota(jnp.int32, shape, 0) == lax.broadcasted_iota(jnp.int32, shape, 1)
    slot_column = jnp.sum(jnp.where(same, slot_ref[...].astype(F32), 0.0), axis=1, keepdims=True)
    hit = slot_column == route_row
    member = dot(one_hot(hit), spread, ((1,), (1,)))
    before = one_hot(
        lax.broadcasted_iota(jnp.int32, (tokens, tokens), 0) < lax.broadcasted_iota(jnp.int32, (tokens, tokens), 1)
    )
    ahead = dot(member.astype(BF16), before)
    place = jnp.where(member > 0.5, ahead, -1.0).astype(BF16)
    place_flat = jnp.where(hit, dot(ahead.astype(BF16), spread), -1.0).astype(BF16)
    return place, place_flat


def prepare(
    plan, groups,
    route_ref, slot_ref, delta_ref, input_ref,
    out_ref,
):
    place, place_flat = places(route_ref, slot_ref)
    slots, rows, dests = plan.group * plan.slots, plan.group * plan.packed, plan.group
    wide_expand = plan.expand(*plan.wide_index(slots))
    wide_rank = plan.rank(plan.wide_index(1)[1])
    dest, _, at = plan.packed_index(slots)
    packed_expand = plan.expand(dest, at)
    _, block, at = plan.packed_index(LANES)
    packed_rank = plan.rank(at)
    low, odd = block < 2, block % 2 == 1
    halves = jnp.concatenate([input_ref[:, : 2 * LANES], input_ref[:, 2 * LANES :]], axis=0)
    for g in range(groups):
        hit = dot(packed_expand, place[g * slots : (g + 1) * slots]) == packed_rank
        chosen = jnp.concatenate([one_hot(hit & low), one_hot(hit & ~low)], axis=1)
        picked = dot(chosen, halves)
        picked = jnp.where(odd, picked[:, LANES:], picked[:, :LANES]).astype(BF16)
        out_ref[g * dests : (g + 1) * dests, : plan.packed, :] = picked.reshape(dests, plan.packed, LANES)
        value = dot(wide_expand, place_flat[g * slots : (g + 1) * slots])
        picked = dot(one_hot(value == wide_rank), delta_ref[...]).astype(BF16)
        out_ref[g * dests : (g + 1) * dests, plan.packed :, :] = picked.reshape(dests, plan.padded, LANES)


def place_at(block, size):
    return pl.ds(pl.multiple_of(block * size, size), size)


def place_of(index_ref, block, size):
    return place_at(index_ref[block], size)


def shared_partial(place_ref, holder_ref, *refs):
    part_refs, (input_ref, weight_ref, all_ref, keep_ref, give_ref, weight_out_ref, sum_ref) = refs[:-7], refs[-7:]
    weight_out_ref[...] = weight_ref[...]
    for m, ref in enumerate(part_refs):
        all_ref[place_of(holder_ref, m, BLOCK), :] = ref[...]
    sum_ref[...] = dot(all_ref[...], input_ref[...], ((0,), (0,)))
    core = place_ref[1]
    for b in range(sum_ref.shape[0] // (2 * BLOCK)):
        at = slice(b * BLOCK, (b + 1) * BLOCK)
        keep_ref[at, :] = sum_ref[place_at(2 * b + core, BLOCK), :]
        give_ref[at, :] = sum_ref[place_at(2 * b + 1 - core, BLOCK), :]


def join_along_y(place_ref, part_ref, weight_ref, *refs):
    out_refs, sum_ref = refs[:-1], refs[-1]
    rows = sum_ref.shape[0]
    total = part_ref[0, :rows, :].astype(F32)
    for y in range(1, part_ref.shape[0]):
        total = total + part_ref[y, :rows, :].astype(F32)
    sum_ref[...] = total
    for y in range(part_ref.shape[0]):
        weight_ref[y * rows : (y + 1) * rows, :] = part_ref[y, rows:, :]
    for step, ref in enumerate(out_refs):
        ref[...] = sum_ref[place_at((place_ref[0] + step) & 3, BLOCK), :]


def shared_rows(plan, groups, place_ref, delta_ref, weight_ref, route_ref, slot_ref, out_ref, chosen_ref, sorted_ref):
    place = places(route_ref, slot_ref)[0]
    slots, rows = plan.group * plan.slots, plan.group * plan.packed
    dest, _, at = plan.packed_index(slots)
    expand = plan.expand(dest, at)
    rank = (lax.broadcasted_iota(jnp.int32, (place.shape[1], rows), 1) % plan.packed % plan.rows % MOST).astype(F32)
    for g in range(groups):
        value = dot(place[g * slots : (g + 1) * slots], expand, ((0,), (1,)))
        chosen_ref[:, g * rows : (g + 1) * rows] = one_hot(value == rank)
    for k in range(weight_ref.shape[0] // BLOCK):
        core, z = place_ref[1] ^ (k % 2), (place_ref[0] - (k // 2) % 4) & 3
        sorted_ref[k * BLOCK : (k + 1) * BLOCK, :] = weight_ref[place_at((core * 8 + k // 8) * 4 + z, BLOCK), :]
    out_ref[...] = dot(delta_ref[...], sorted_ref[...])


def arrange(plan, groups, arrived_ref, shared_ref, *refs):
    weight_refs, (delta_ref, part_ref) = refs[:-2], refs[-2:]
    sort = plan.slot_from_wide()
    part = plan.slot_rows
    for g in range(groups):
        wide = arrived_ref[g * plan.group : (g + 1) * plan.group, plan.packed :, :]
        wide = dot(sort, wide.reshape(plan.group * plan.padded, LANES)).astype(BF16)
        for s in range(plan.slots):
            delta_ref[s, g * part : (g + 1) * part, :] = wide[s * part : (s + 1) * part]
    count = part_ref.shape[0]
    rows = shared_ref.shape[0] // count
    for y in range(count):
        at = slice(y * rows, (y + 1) * rows)
        part_ref[y, :rows, :] = shared_ref[at, :]
        for step, ref in enumerate(weight_refs):
            part_ref[y, rows + step * BLOCK : rows + (step + 1) * BLOCK, :] = ref[...]


def project_early(plan, late, index_ref, *refs):
    delta_refs, (weight_ref, out_ref, late_ref, kept_at, sorted_ref, sems) = refs[:-6], refs[-6:]
    copies = started([(ref, kept_at.at[m]) for m, ref in enumerate(delta_refs)], sems)
    count = len(delta_refs)
    for s in range(plan.slots):
        for m in range(count):
            sorted_ref[s, m * LANES : (m + 1) * LANES, :] = weight_ref[s, place_of(index_ref, m, LANES), :]
        for m in range(late):
            late_ref[s, m * LANES : (m + 1) * LANES, :] = weight_ref[s, place_of(index_ref, count + m, LANES), :]
        out_ref[s] = dot(jnp.concatenate([ref[s] for ref in delta_refs], axis=1), sorted_ref[s])
    for copy in copies:
        copy.wait()


def project(plan, groups, *refs):
    delta_refs, (weight_ref, early_ref, out_ref, kept_at, value_ref, sems) = refs[:-6], refs[-6:]
    copies = started([(ref, kept_at.at[m]) for m, ref in enumerate(delta_refs)], sems)
    rows, part = plan.group * plan.packed, plan.slot_rows
    for s in range(plan.slots):
        value = dot(jnp.concatenate([ref[s] for ref in delta_refs], axis=1), weight_ref[s])
        value_ref[s] = (early_ref[s] + value).astype(BF16)
    unsort = plan.packed_from_slot()
    block = plan.packed_index(LANES)[1]
    for g in range(groups):
        value = jnp.concatenate([value_ref[s, g * part : (g + 1) * part, :] for s in range(plan.slots)], axis=0)
        out_ref[g * rows : (g + 1) * rows, :] = by_block(plan, dot(unsort, value), block)
    for copy in copies:
        copy.wait()


def weight_gradient(plan, groups, index_ref, early_ref, late_ref, input_ref, out_ref, sorted_ref):
    rows, part = plan.group * plan.packed, plan.slot_rows
    unsort = plan.packed_from_slot()
    mask = plan.block_mask()
    for g in range(groups):
        packed = input_ref[g * plan.group : (g + 1) * plan.group, : plan.packed, :].reshape(rows, LANES)
        wide = dot(unsort, widened(plan, packed, mask), ((0,), (0,))).astype(BF16)
        for s in range(plan.slots):
            sorted_ref[s, g * part : (g + 1) * part, :] = wide[s * part : (s + 1) * part]
    for s in range(plan.slots):
        parts = [ref[m, s] for ref in (early_ref, late_ref) for m in range(ref.shape[0])]
        delta = jnp.concatenate(parts, axis=1)
        value = dot(delta, sorted_ref[s], ((0,), (0,))).astype(BF16)
        for m in range(len(parts)):
            out_ref[s, place_of(index_ref, m, LANES), :] = value[m * LANES : (m + 1) * LANES]


def combine(plan, groups, returned_ref, chosen_ref, shared_ref, *refs):
    part_refs, (out_ref, sum_ref) = refs[:4], refs[4:]
    rows = plan.group * plan.packed
    mask = plan.block_mask()
    total = shared_ref[...]
    for g in range(groups):
        at = slice(g * rows, (g + 1) * rows)
        total = total + dot(chosen_ref[:, at], widened(plan, returned_ref[at, :], mask))
    out_ref[...] = total.astype(BF16)
    sum_ref[...] = part_refs[0][...] + part_refs[1][...] + part_refs[2][...] + part_refs[3][...]


def moved(block, axis, target):
    return lax.ppermute(block, axis, [(i, target(i)) for i in range(lax.axis_size(axis))])


def along_x(distance):
    return lambda i: (i & 4) | ((i + distance) & 3)


def other_z(i):
    return i ^ 4


def along_z(distance):
    return lambda i: (i & ~6) | ((i + 2 * distance) & 6)


def other_core(i):
    return i ^ 1


def to_right(block):
    return moved(block, "tensor", along_x(1))


def to_left(block):
    return moved(block, "tensor", along_x(-1))


def body(layer_input, routed_delta, shared_delta, expert_weight, shared_weight, routing, slot_expert):
    tokens, top = routing.shape
    slots, hidden, columns = expert_weight.shape
    shared_hidden = shared_delta.shape[1]
    dp_count = lax.axis_size("dp")
    group = 8
    groups = dp_count // group
    plan = Plan(slots, columns, group)
    packed_rows = dp_count * plan.packed
    mine = lax.axis_index("dp")
    my_place = jnp.stack([(mine >> 1) & 3, mine & 1])
    along_y = [[8 * y + r for y in range(dp_count // 8)] for r in range(8)]
    own = lax.axis_index("tensor")
    holders = jnp.stack([(own & 4) ^ flip | ((own + step) & 3) for step in (0, -1, 1, 2) for flip in (0, 4)])
    value_rows = pltpu.VMEM((slots, dp_count * MOST, columns), BF16)

    def exchanged(block, groups=None):
        return lax.all_to_all(block, "dp", split_axis=0, concat_axis=0, axis_index_groups=groups, tiled=True)

    sent = call(
        functools.partial(prepare, plan, groups),
        jax.ShapeDtypeStruct((dp_count, plan.packed + plan.padded, LANES), BF16),
        routing.T,
        slot_expert.reshape(1, -1),
        routed_delta.reshape(tokens * top, LANES),
        layer_input,
    )
    sent, other_delta = ready(sent, moved(shared_delta, "tensor", other_z))
    arrived = exchanged(sent)

    pair = (shared_delta, other_delta)
    shared_all, keep, give, own_weight = call(
        shared_partial,
        (
            jax.ShapeDtypeStruct((tokens, shared_hidden), BF16),
            jax.ShapeDtypeStruct((shared_hidden // 2, columns), F32),
            jax.ShapeDtypeStruct((shared_hidden // 2, columns), F32),
            jax.ShapeDtypeStruct(shared_weight.shape, BF16),
        ),
        *pair,
        *[to_right(part) for part in pair],
        *[to_left(part) for part in pair],
        *[moved(part, "tensor", along_x(2)) for part in pair],
        layer_input,
        shared_weight,
        index=(my_place, holders),
        scratch=[pltpu.VMEM((shared_hidden, columns), F32)],
    )
    shared_part = (keep + moved(give, "dp", other_core)).astype(BF16)
    weights = [own_weight] + [moved(own_weight, "dp", along_z(step)) for step in (1, 2, 3)]

    own_deltas, parts = call(
        functools.partial(arrange, plan, groups),
        (
            jax.ShapeDtypeStruct((slots, dp_count * MOST, LANES), BF16),
            jax.ShapeDtypeStruct((8, 8 * BLOCK, columns), BF16),
        ),
        arrived,
        shared_part,
        *weights,
    )
    partner_deltas = moved(own_deltas, "tensor", other_z)
    own_left, own_right = to_right(own_deltas), to_left(own_deltas)
    partner_left, partner_right = to_right(partner_deltas), to_left(partner_deltas)
    deltas = [
        own_deltas,
        partner_deltas,
        own_left,
        partner_left,
        own_right,
        partner_right,
        to_right(own_left),
        to_left(partner_right),
    ]
    parts = exchanged(parts, along_y)
    early, late = deltas[:6], deltas[6:]
    early_rows, late_weight, kept_early = call(
        functools.partial(project_early, plan, len(late)),
        (
            jax.ShapeDtypeStruct((slots, dp_count * MOST, columns), F32),
            jax.ShapeDtypeStruct((slots, len(late) * LANES, columns), BF16),
            jax.ShapeDtypeStruct((len(early),) + own_deltas.shape, BF16),
        ),
        *early,
        expert_weight,
        index=(holders,),
        scratch=[
            pltpu.VMEM((slots, len(early) * LANES, columns), BF16),
            pltpu.SemaphoreType.DMA((len(early),)),
        ],
        out_specs=(IN_VMEM, IN_VMEM, ANYWHERE),
    )
    outgoing, kept_late = call(
        functools.partial(project, plan, groups),
        (
            jax.ShapeDtypeStruct((packed_rows, LANES), BF16),
            jax.ShapeDtypeStruct((len(late),) + own_deltas.shape, BF16),
        ),
        *late,
        late_weight,
        early_rows,
        scratch=[value_rows, pltpu.SemaphoreType.DMA((len(late),))],
        out_specs=(IN_VMEM, ANYWHERE),
    )

    returned = exchanged(outgoing.reshape(dp_count, plan.packed, LANES)).reshape(packed_rows, LANES)
    expert_gradient = call(
        functools.partial(weight_gradient, plan, groups),
        jax.ShapeDtypeStruct(expert_weight.shape, BF16),
        kept_early,
        kept_late,
        arrived,
        index=(holders,),
        scratch=[value_rows],
    )
    weight_part, *shared_parts = call(
        join_along_y,
        (jax.ShapeDtypeStruct((32 * BLOCK, columns), BF16),)
        + tuple(jax.ShapeDtypeStruct((BLOCK, columns), F32) for _ in range(4)),
        parts,
        index=(my_place,),
        scratch=[pltpu.VMEM((4 * BLOCK, columns), F32)],
    )
    weight_all = jnp.concatenate([weight_part, moved(weight_part, "dp", other_core)], axis=0)
    shared_term, chosen = call(
        functools.partial(shared_rows, plan, groups),
        (jax.ShapeDtypeStruct((tokens, columns), F32), jax.ShapeDtypeStruct((tokens, packed_rows), BF16)),
        shared_all,
        weight_all,
        routing.T,
        slot_expert.reshape(1, -1),
        index=(my_place,),
        scratch=[pltpu.VMEM((shared_hidden, columns), BF16)],
        after=(expert_gradient,),
    )
    shared_parts = shared_parts[:1] + [
        moved(part, "dp", along_z(step)) for step, part in enumerate(shared_parts) if step
    ]
    input_gradient, shared_gradient = call(
        functools.partial(combine, plan, groups),
        (
            jax.ShapeDtypeStruct((tokens, columns), BF16),
            jax.ShapeDtypeStruct(shared_weight.shape, F32),
        ),
        returned,
        chosen,
        shared_term,
        *shared_parts,
    )
    return input_gradient, expert_gradient, shared_gradient


def solution(mesh):
    return jax.shard_map(
        body,
        mesh=mesh,
        in_specs=(
            P("dp", "tensor"),
            P("dp", None, "tensor"),
            P(("dp", "tensor"), None),
            P("dp", None, "tensor"),
            P("dp", "tensor"),
            P("dp", None),
            P(),
        ),
        out_specs=(P("dp", "tensor"), P("dp", None, "tensor"), P("dp", "tensor")),
        check_vma=False,
    )
```
